128 devices in a mesh: blk: 8 (over x_hi, y), occ: 16 (over z, x_lo, core).
Axes of the slice: x: 4 (x_hi: 2, x_lo: 2; x = x_hi * 2 + x_lo), y: 4, z: 4, core: 2. Of those that a mesh axis runs over, the one named last changes fastest.
Arguments:
- tiles: bfloat16 [131072, 128], P(('blk', 'occ')), may hold values from -1.5 to 1.5
- owner: int32 [131072, 1], P(('blk', 'occ')), may hold values from 0 to 15; in each aligned block of 1024 rows (0 to 1023, 1024 to 2047, ...) at most 128 rows name the same one
- sub_block: int32 [131072], P(('blk', 'occ')), may hold values from 0 to 1
- fit_ac: bfloat16 [32, 40, 6400], P(None, None, 'occ'), may hold values from -0.29882812 to 0.29882812
- fit_bd: bfloat16 [128, 128, 6400], P('blk', None, 'occ'), may hold values from -0.29882812 to 0.29882812
Outputs:
- ladder: bfloat16 [8192, 5120], P(('blk', 'occ'))
The draws below stay inside these ranges and needn't reach their ends.
Inputs may be any that keep to these rules, and one draw needn't show every extreme that they name: Among the 1024 tiles of one device (aligned blocks), no owner is named more than 128 times, and in every draw some owner is named exactly 128 times by some device.
All inputs are finite; a program needn't handle non-finite values.
Results may differ from the reference program's by a relative error of at most 0.005.
Values may be sent and summed in bfloat16 or wider, within the bound.
A program may use at most 192 MiB of HBM per device.

```python
import math
import jax
import jax.numpy as jnp
import numpy as np
from jax import lax

NA = 40
NB = 128
NC = 32
ND = 128
NQ = 6400
TILES_PAIR = 16
ROWS_DEV = 1024
GROUPS = 16
BLOCKS_OWNER = 2
CAP = 128
ROWS = 131072
PAIRS = 8192


def with_ends(array, key, smallest, top_value):
    longest = array.shape.index(max(array.shape))
    spots = []
    for shift in (0, 1):
        where = [jax.random.randint(jax.random.fold_in(key, axis), (), 0, length) for axis, length in enumerate(array.shape)]
        where[longest] = (where[longest] + shift) % array.shape[longest]
        spots.append(tuple(where))
    return array.at[spots[0]].set(smallest).at[spots[1]].set(top_value)


def with_spikes(array, stream_key, source, target, blocks, factor):
    def block_of(axis_at):
        return (jnp.arange(array.shape[axis_at]) // (array.shape[axis_at] // blocks)).reshape((-1,) + (1,) * (array.ndim - 1 - axis_at))

    first = jax.random.permutation(stream_key, blocks)[block_of(target)]
    second = (block_of(target) + blocks // 2) % blocks
    return jnp.where((block_of(source) == first) | (block_of(source) == second), factor * array, array)


def levels(key, shape, cuts, least, top_value):
    gain = 1.0
    for axis_at, blocks in cuts:
        draws = jax.random.uniform(jax.random.fold_in(jax.random.fold_in(key, 6), axis_at), (blocks,), jnp.float32, least / len(cuts), top_value / len(cuts))
        gain = gain * jnp.repeat(jnp.exp(draws), shape[axis_at] // blocks).reshape((-1,) + (1,) * (len(shape) - 1 - axis_at))
    return gain


def routed_block(key, own, number, rows, number_of, top, reach, slope):
    order = jax.random.permutation(key, number_of)
    heavy_load, common = portions_of(number_of, rows * top, reach, slope, True), portions_of(number_of, rows * top, reach, slope, False)
    places = jnp.arange(number_of)

    def named(lengths, rotation):
        used = int((lengths > 0).sum())
        fixed = max(1, used // 4)
        shifted = fixed + (places - fixed + rotation * (used - fixed)) % max(1, number_of - fixed)
        return jnp.zeros((number_of,), jnp.int32).at[order[jnp.where(places < fixed, places, shifted)]].set(jnp.asarray(lengths, jnp.int32))

    lengths = jnp.where(number % 4 == 0, named(heavy_load, number // 4), named(common, number - number // 4 - 1))
    mixed = jax.random.permutation(jax.random.fold_in(own, 3), number_of)
    source_of, sink = mixed[0:number_of // 2 * 2:2], mixed[1:number_of // 2 * 2:2]
    slack = jnp.minimum(lengths[source_of] - 1, reach - lengths[sink]) // 2
    slack = jnp.where((source_of == order[0]) | (sink == order[0]) | (lengths[sink] == 0), 0, jnp.maximum(slack, 0))
    shifted = jax.random.randint(jax.random.fold_in(own, 4), (number_of // 2,), 0, 1 << 20) % (slack + 1)
    lengths = lengths.at[source_of].add(-shifted).at[sink].add(shifted)
    items = jnp.searchsorted(jnp.cumsum(lengths), jnp.arange(rows * top), side="right").astype(jnp.int32)
    listing = items.reshape(top, rows).T
    listing = listing[jax.random.permutation(jax.random.fold_in(own, 1), rows)]
    rotation = jax.random.randint(jax.random.fold_in(own, 2), (rows, 1), 0, top)
    return jnp.take_along_axis(listing, (jnp.arange(top)[None, :] + rotation) % top, axis=1)


def portions_of(number_of, total, bound, lean, full):
    portions = [(1 << 20) // math.isqrt(grade ** lean) + 1 for grade in range(1, number_of + 1)]
    largest = bound if full else min(bound, max(-(-total // number_of), total * portions[0] // sum(portions)))
    least = 1 if total - largest >= number_of - 1 else 0
    holding, surplus = [largest] + [least] * (number_of - 1), total - largest - least * (number_of - 1)
    while surplus > 0:
        free = [i for i in range(1, number_of) if holding[i] < largest] or [i for i in range(1, number_of) if holding[i] < bound]
        whole, budget = sum([portions[i] for i in free]), surplus
        for i in free:
            more = min(bound - holding[i], max(1, budget * portions[i] // whole), surplus)
            holding[i] = holding[i] + more
            surplus = surplus - more
    return np.array(holding)


def centred(rng, extent, scale, most, split=(), kind=jnp.bfloat16):
    values = scale * jax.random.normal(rng, extent, jnp.float32)
    if split:
        values = values * levels(rng, extent, split, -0.22, 0.18)
    return jnp.clip(values, -most, most).astype(kind)


def bell_draw_with(key, dims, scale, reach, split, heavy, kind=jnp.bfloat16):
    entries = scale * jax.random.normal(key, dims, jnp.float32)
    if split:
        entries = entries * levels(key, dims, split, -0.22, 0.18)
    return jnp.clip(with_spikes(entries, jax.random.fold_in(key, 3), *heavy), -reach, reach).astype(kind)


def setup_inputs(seed: int = 0) -> dict:
    arg_keys = jax.random.split(jax.random.key(seed), 6)
    tiles = centred(arg_keys[0], (ROWS, ND), 0.25, 1.5, ((0, 128),))
    owner_keys = jax.random.split(jax.random.fold_in(arg_keys[1], 1), ROWS // ROWS_DEV)
    owner_turns = jax.random.permutation(jax.random.fold_in(arg_keys[1], 3), ROWS // ROWS_DEV)
    owner = jax.vmap(lambda own, number: routed_block(jax.random.fold_in(arg_keys[1], 2), own, number, ROWS_DEV, GROUPS, 1, CAP, 2))(owner_keys, owner_turns).reshape((ROWS, 1))
    sub_block = with_ends(jax.random.randint(arg_keys[2], (ROWS,), 0, BLOCKS_OWNER), jax.random.fold_in(arg_keys[2], 1), 0, BLOCKS_OWNER - 1).astype(jnp.int32)
    fit_ac = bell_draw_with(arg_keys[3], (NC, NA, NQ), 0.05, 0.29882812, ((2, 16),), (2, 0, 16, 2.0))
    fit_bd = centred(arg_keys[4], (NB, ND, NQ), 0.05, 0.29882812, ((0, 8), (2, 16)))
    return dict(tiles=tiles, owner=owner, sub_block=sub_block, fit_ac=fit_ac, fit_bd=fit_bd)


def reference(tiles, owner, sub_block, fit_ac, fit_bd):
    block = (owner[:, 0] * (NC // GROUPS) + sub_block).astype(jnp.int32)
    pair = (jnp.arange(ROWS, dtype=jnp.int32) // TILES_PAIR).astype(jnp.int32)
    segment = (pair * NC + block).astype(jnp.int32)
    summed = jax.ops.segment_sum(tiles.astype(jnp.float32), segment, num_segments=PAIRS * NC)
    summed = summed.reshape(PAIRS, NC * ND)
    left_panel = fit_ac.reshape(NC * NA, NQ)
    right_panel = fit_bd.reshape(NB * ND, NQ)
    integral_full = lax.dot_general(left_panel, right_panel, (((1,), (1,)), ((), ())), preferred_element_type=jnp.float32)
    integral_full = integral_full.astype(jnp.bfloat16).reshape(NC, NA, NB, ND)
    integral_full = integral_full.transpose(0, 3, 1, 2).reshape(NC * ND, NA * NB).astype(jnp.float32)
    result = jnp.dot(summed, integral_full, precision=lax.Precision.HIGHEST, preferred_element_type=jnp.float32)
    return result.astype(jnp.bfloat16)
```

```python
import jax
import jax.numpy as jnp
from jax import lax
from jax.experimental import pallas as pl
from jax.experimental.pallas import tpu as pltpu
from jax.sharding import PartitionSpec as P

MESH = pl.DeviceIdType.MESH
RING = 4
CORES = 2
SLICES = 2
TILES_PAIR = 16
NA, NB, NC, ND = 40, 128, 32, 128
BLOCKS_OWNER = 2
PLANE = RING * RING
A_HALF = NA // 2
C_PART = NC // RING
ROWS = C_PART * NA
B_CORE = 8
WIDE = 2 * ND
K_HALF = C_PART * ND // 2
OUT_ROWS = 2 * NA
STEP = 256

F32, BF16 = jnp.float32, jnp.bfloat16


def product(left, right, right_axis):
    return lax.dot_general(left, right, (((1,), (right_axis,)), ((), ())), preferred_element_type=F32)


def kernel(
    tiles, labels, fit_a, fit_b, out,
    a_own, a_mate, b_own, b_mate, slots, far_out, side_out, comb_out, far_in, side_in, comb_in,
    keep_comb, keep_own, x_out, x_in, arranged, ints, summed, total, parcels, got, names, final,
    load_sem, mate_s, mate_r, ring1_s, ring1_r, half1_s, half1_r, ring2_s, ring2_r, pass2_s, pass2_r,
    far_s, far_r, side_s, side_r, comb_s, comb_r, x_s, x_r, ag_s, ag_r, fw_s, fw_r, cx_s, cx_r, out_s, out_r,
):
    blk, occ = lax.axis_index("blk"), lax.axis_index("occ")
    x_hi, y = lax.div(blk, RING), lax.rem(blk, RING)
    z, x_lo, k = lax.div(occ, 4), lax.rem(lax.div(occ, 2), 2), lax.rem(occ, 2)
    x = x_hi * 2 + x_lo
    rows_dev = tiles.shape[0]
    pairs_dev = rows_dev // TILES_PAIR

    def mod(value):
        return lax.rem(value, RING)

    def device(x_at, y_at, z_at, k_at):
        return (lax.div(x_at, 2) * RING + y_at, z_at * 4 + lax.rem(x_at, 2) * 2 + k_at)

    up, down, far = mod(z + 1), mod(z + 3), mod(z + 2)
    mate = device(x, y, z, 1 - k)
    partner = device(x_hi * 2 + 1 - x_lo, y, z, k)

    def along(d):
        return device(x, y, mod(z + 1 + 2 * d), k)

    me = x * RING + y
    u, v = (1 - k) * x + k * y, (1 - k) * y + k * x

    def slot_of(u_at, v_at):
        return ((1 - k) * u_at + k * v_at) * RING + (1 - k) * v_at + k * u_at

    def plane_device(u_at, v_at):
        return device((1 - k) * u_at + k * v_at, (1 - k) * v_at + k * u_at, z, k)

    def remote(src, dst, send, recv, to):
        return pltpu.make_async_remote_copy(
            src_ref=src, dst_ref=dst, send_sem=send, recv_sem=recv, device_id=to, device_id_type=MESH
        )

    def arrival(dst, send, recv):
        remote(dst, dst, send, recv, mate).wait_recv()

    load_a = pltpu.make_async_copy(fit_a, a_own, load_sem.at[0])
    load_b = pltpu.make_async_copy(fit_b.at[pl.ds(k * B_CORE, B_CORE)], b_own, load_sem.at[1])
    load_t = pltpu.make_async_copy(tiles, slots.at[me, pl.ds(0, rows_dev)], load_sem.at[2])
    load_l = pltpu.make_async_copy(labels, slots.at[me, pl.ds(rows_dev, 16)], load_sem.at[3])
    for load in (load_t, load_l, load_a, load_b):
        load.start()

    barrier = pltpu.get_barrier_semaphore()

    def greet(i, carry):
        to = device(mod(x + lax.div(i, RING)), mod(y + lax.rem(i, RING)), z, k)
        pl.semaphore_signal(barrier, inc=1, device_id=to, device_id_type=MESH)
        return carry

    for to in (mate, along(0), along(1)):
        pl.semaphore_signal(barrier, inc=1, device_id=to, device_id_type=MESH)
    lax.fori_loop(1, PLANE, greet, 0)
    pl.semaphore_wait(barrier, PLANE + 2)

    swap_a = remote(fit_a, a_mate, mate_s.at[0], mate_r.at[0], mate)
    swap_b = remote(fit_b.at[pl.ds((1 - k) * B_CORE, B_CORE)], b_mate, mate_s.at[1], mate_r.at[1], mate)
    swap_b.start()
    swap_a.start()
    load_t.wait()
    load_l.wait()

    def ring1(d):
        return remote(slots.at[me], slots.at[me], ring1_s.at[d], ring1_r.at[d], plane_device(mod(u + 1 + 2 * d), v))

    def part1(d, slot):
        start, size = (0, rows_dev // 2) if d == 0 else (rows_dev // 2, rows_dev // 2 + 16)
        return slots.at[slot, pl.ds(start, size)]

    def half1(d, back):
        ref = part1(d, slot_of(mod(u + back), v))
        return remote(ref, ref, half1_s.at[d], half1_r.at[d], plane_device(mod(u + 1 + 2 * d), v))

    def ring2(d, i):
        ref = slots.at[slot_of(mod(u + i), v)]
        return remote(ref, ref, ring2_s.at[d, i], ring2_r.at[d, i], plane_device(u, mod(v + 1 + 2 * d)))

    def pass2(i):
        d = i // 2
        ref = slots.at[slot_of(mod(u + i), mod(v + 3 - 2 * d))]
        return remote(ref, ref, pass2_s.at[i], pass2_r.at[i], plane_device(u, mod(v + 1 + 2 * d)))

    ring1(0).start()
    ring1(1).start()
    load_a.wait()
    load_b.wait()
    swap_b.wait_recv()
    swap_a.wait_recv()

    def partial(part, h, s):
        rows = pl.ds(pl.multiple_of(part * ROWS, ROWS), ROWS)
        b = h * 4 + s * 2
        own = product(a_own[rows, :], jnp.concatenate([b_own[b], b_own[b + 1]], axis=1), 0)
        return own + product(a_mate[rows, :], jnp.concatenate([b_mate[b], b_mate[b + 1]], axis=1), 0)

    def far_copy(s, d):
        return remote(far_out.at[s, d], far_in.at[s, d], far_s.at[s, d], far_r.at[s, d], along(d))

    def side_copy(s, d):
        return remote(side_out.at[s, d], side_in.at[s, d], side_s.at[s, d], side_r.at[s, d], along(d))

    def comb_copy(s, d):
        return remote(comb_out.at[s, d], comb_in.at[s, d], comb_s.at[s, d], comb_r.at[s, d], along(d))

    def x_copy(s):
        return remote(x_out.at[s], x_in.at[s], x_s.at[s], x_r.at[s], partner)

    def send_far(i, carry):
        s, d = lax.div(i, 2), lax.rem(i, 2)
        far_out[s, d] = partial(far, d, s).astype(BF16)
        far_copy(s, d).start()
        return carry

    def send_side(i, carry):
        s, d = lax.div(i, 2), lax.rem(i, 2)
        side_out[s, d] = partial(mod(z + 1 + 2 * d), 1 - d, s).astype(BF16)
        side_copy(s, d).start()
        return carry

    def make_keep(i, carry):
        s, d = lax.div(i, 2), lax.rem(i, 2)
        keep_comb[s, d] = partial(mod(z + 1 + 2 * d), d, s)
        return carry

    def make_own(i, carry):
        s, h = lax.div(i, 2), lax.rem(i, 2)
        keep_own[s, h] = partial(z, h, s)
        return carry

    lax.fori_loop(0, 4, send_far, 0)
    lax.fori_loop(0, 4, send_side, 0)

    arrival(slots.at[slot_of(mod(u + 3), v)], ring1_s.at[0], ring1_r.at[0])
    half1(0, 3).start()
    arrival(slots.at[slot_of(mod(u + 1), v)], ring1_s.at[1], ring1_r.at[1])
    half1(1, 1).start()
    for i in (0, 1, 3):
        for d in (0, 1):
            ring2(d, i).start()

    lax.fori_loop(0, 4, make_keep, 0)
    lax.fori_loop(0, 4, make_own, 0)

    def send_comb(s):
        for d in (0, 1):
            far_copy(s, d).wait_recv()
            comb_out[s, d] = (keep_comb[s, d] + far_in[s, d].astype(F32)).astype(BF16)
            comb_copy(s, d).start()

    send_comb(0)
    arrival(part1(0, slot_of(mod(u + 2), v)), half1_s.at[0], half1_r.at[0])
    arrival(part1(1, slot_of(mod(u + 2), v)), half1_s.at[1], half1_r.at[1])
    for d in (0, 1):
        ring2(d, 2).start()
    send_comb(1)

    def build(slot):
        names[...] = slots[slot, pl.ds(rows_dev, 16), :].astype(F32)

        def one(j, carry):
            label = jnp.concatenate([names[pl.ds(2 * j, 1), :], names[pl.ds(2 * j + 1, 1), :]], axis=1)
            pair = lax.div(lax.broadcasted_iota(jnp.int32, (1, STEP), 1), TILES_PAIR)
            spot = label.astype(jnp.int32) * 16 + pair
            choice = lax.broadcasted_iota(jnp.int32, (NC * 16, STEP), 0) == spot
            values = slots[slot, pl.ds(pl.multiple_of(j * STEP, STEP), STEP), :]
            sums = product(jnp.where(choice, 1.0, 0.0).astype(BF16), values, 0).astype(BF16)
            rows = pl.ds(pl.multiple_of(slot * pairs_dev + j * 16, 16), 16)
            for c in range(NC):
                summed[c // 4, rows, (c % 4) * ND : (c % 4 + 1) * ND] = sums[c * 16 : (c + 1) * 16, :]
            return carry

        lax.fori_loop(0, rows_dev // STEP, one, 0)

    def build_line(v_at):
        def one(i, carry):
            build(slot_of(i, v_at))
            return carry

        lax.fori_loop(0, RING, one, 0)

    def send_x(s):
        comb_copy(s, 0).wait_recv()
        comb_copy(s, 1).wait_recv()
        side_copy(s, 0).wait_recv()
        side_copy(s, 1).wait_recv()
        h = 1 - x_lo
        x_out[s] = (keep_own[s, h] + comb_in[s, h].astype(F32) + side_in[s, 1 - h].astype(F32)).astype(BF16)
        x_copy(s).start()

    def ag_copy(s, d):
        ref = ints.at[s, z, k]
        return remote(ref, ref, ag_s.at[s, d], ag_r.at[s, d], along(d))

    def fw_copy(s, d):
        ref = ints.at[s, mod(z + 3 - 2 * d), k, d]
        return remote(ref, ref, fw_s.at[s, d], fw_r.at[s, d], along(d))

    def cx_ref(s, i, core):
        if i < 3:
            return ints.at[s, (z, down, up)[i], core]
        return ints.at[s, far, core, i - 3]

    def cx_copy(s, i):
        ref = cx_ref(s, i, k)
        return remote(ref, ref, cx_s.at[s, i], cx_r.at[s, i], mate)

    def finish(s):
        x_copy(s).wait_recv()
        h = x_lo
        for two in range(C_PART // 2):
            rows = pl.ds(two * 2 * NA, 2 * NA)
            value = (
                keep_own[s, h, rows, :]
                + comb_in[s, h, rows, :].astype(F32)
                + side_in[s, 1 - h, rows, :].astype(F32)
                + x_in[s, rows, :].astype(F32)
            )
            for one in range(2):
                columns = pl.ds((two * 2 + one) * ND, ND)
                for b in range(2):
                    block = value[one * NA : (one + 1) * NA, b * ND : (b + 1) * ND]
                    arranged[pl.ds(b * A_HALF, A_HALF), columns] = block[:A_HALF]
                    arranged[pl.ds(NA + b * A_HALF, A_HALF), columns] = block[A_HALF:]
        for half in range(2):
            ints[s, z, k, half] = arranged[:, half * K_HALF : (half + 1) * K_HALF].astype(BF16)
        ag_copy(s, 0).start()
        ag_copy(s, 1).start()
        cx_copy(s, 0).start()

    build_line(v)
    send_x(0)

    for i in range(RING):
        arrival(slots.at[slot_of(mod(u + i), mod(v + 3))], ring2_s.at[0, i], ring2_r.at[0, i])
        if i < 2:
            pass2(i).start()
    finish(0)
    for i in range(RING):
        arrival(slots.at[slot_of(mod(u + i), mod(v + 1))], ring2_s.at[1, i], ring2_r.at[1, i])
        if i >= 2:
            pass2(i).start()
    build_line(mod(v + 3))
    send_x(1)

    def forward(s):
        for d in (0, 1):
            from_z = mod(z + 3 - 2 * d)
            arrival(ints.at[s, from_z, k], ag_s.at[s, d], ag_r.at[s, d])
            fw_copy(s, d).start()
            cx_copy(s, 1 + d).start()

    def last_forward(s):
        for d in (0, 1):
            arrival(ints.at[s, far, k, d], fw_s.at[s, d], fw_r.at[s, d])
            cx_copy(s, 3 + d).start()

    forward(0)
    finish(1)
    build_line(mod(v + 1))
    for i in range(RING):
        arrival(slots.at[slot_of(mod(u + i), mod(v + 2))], pass2_s.at[i], pass2_r.at[i])
    build_line(mod(v + 2))

    def multiply(s, part, half, first):
        left = jnp.concatenate([ints[s, part, 0, half], ints[s, part, 1, half]], axis=0)

        def one(n, carry):
            right = summed[part * 2 + half, pl.ds(pl.multiple_of(n * STEP, STEP), STEP), :]
            value = product(left, right, 1)
            total[s, n] = value if first else total[s, n] + value
            return carry

        lax.fori_loop(0, RING, one, 0)

    def gathered(s, i):
        arrival(cx_ref(s, i, 1 - k), cx_s.at[s, i], cx_r.at[s, i])
        if i < 3:
            part = (z, down, up)[i]
            multiply(s, part, 0, i == 0)
            multiply(s, part, 1, False)
        else:
            multiply(s, far, i - 3, False)

    def out_copy(s, i):
        x_at, y_at = mod(x + lax.div(i, RING)), mod(y + lax.rem(i, RING))
        return remote(
            parcels.at[s, x_at * RING + y_at], got.at[s, me], out_s.at[s, i], out_r.at[s, i], device(x_at, y_at, z, k)
        )

    def send_out(s):
        low = lax.broadcasted_iota(jnp.int32, (OUT_ROWS, 128), 1) < 64

        def pack(n, carry):
            for q in range(2):
                value = total[s, n, :, q * 128 : (q + 1) * 128]
                top = jnp.concatenate([value[0:NA], value[2 * NA : 3 * NA]], axis=0)
                bottom = jnp.concatenate([value[NA : 2 * NA], value[3 * NA : 4 * NA]], axis=0)
                first = jnp.where(low, top, pltpu.roll(bottom, 64, 1))
                second = jnp.where(low, pltpu.roll(top, 64, 1), bottom)
                parcels[s, n * RING + 2 * q] = first.astype(BF16)
                parcels[s, n * RING + 2 * q + 1] = second.astype(BF16)
            return carry

        def send(i, carry):
            out_copy(s, i).start()
            return carry

        lax.fori_loop(0, RING, pack, 0)
        lax.fori_loop(1, PLANE, send, 0)

    def unpack(s, x_at, y_at, value):
        base = (lax.div(x_at, 2) * RING + y_at) * 16 + lax.rem(x_at, 2) * 4 + s * 2
        for core in range(CORES):
            rows = pl.ds(pl.multiple_of((base + core * 8) * A_HALF, 8), NA)
            final[rows, :] = value[core * NA : (core + 1) * NA]

    def receive(s):
        unpack(s, x, y, parcels[s, me].astype(F32))

        def one(i, carry):
            x_at, y_at = mod(x + RING - lax.div(i, RING)), mod(y + RING - lax.rem(i, RING))
            slot = x_at * RING + y_at
            arrival(got.at[s, slot], out_s.at[s, i], out_r.at[s, i])
            unpack(s, x_at, y_at, got[s, slot].astype(F32))
            return carry

        lax.fori_loop(1, PLANE, one, 0)

    for i in range(3):
        gathered(0, i)
    last_forward(0)
    forward(1)
    for i in range(3, 5):
        gathered(0, i)
    send_out(0)
    for i in range(3):
        gathered(1, i)
    last_forward(1)
    for i in range(3, 5):
        gathered(1, i)
    send_out(1)
    receive(0)
    receive(1)
    for i in range(A_HALF):
        value = final[pl.ds(i, NB, stride=A_HALF), :]
        turned = value.T.astype(BF16)
        out[:, i * NB : (i + 1) * NB] = turned[:pairs_dev]
        out[:, (i + A_HALF) * NB : (i + A_HALF + 1) * NB] = turned[pairs_dev:]

    swap_a.wait_send()
    swap_b.wait_send()
    for d in (0, 1):
        ring1(d).wait_send()
        half1(d, 3 - 2 * d).wait_send()
        for i in range(RING):
            ring2(d, i).wait_send()
    for i in range(RING):
        pass2(i).wait_send()
    for s in range(SLICES):
        x_copy(s).wait_send()
        for d in (0, 1):
            far_copy(s, d).wait_send()
            side_copy(s, d).wait_send()
            comb_copy(s, d).wait_send()
            ag_copy(s, d).wait_send()
            fw_copy(s, d).wait_send()
        for i in range(5):
            cx_copy(s, i).wait_send()

        def sent(i, carry):
            out_copy(s, i).wait_send()
            return carry

        lax.fori_loop(1, PLANE, sent, 0)


def on_device(tiles, owner, sub_block, fit_ac, fit_bd):
    rows_dev = tiles.shape[0]
    depth = fit_ac.shape[2]
    labels = (owner[:, 0] * BLOCKS_OWNER + sub_block).reshape(rows_dev // 128, 128).astype(BF16)
    labels = jnp.pad(labels, ((0, 16 - rows_dev // 128), (0, 0)))
    fit_a = fit_ac.reshape(NC * NA, depth)
    fit_b = jnp.swapaxes(fit_bd, 1, 2)
    pairs = rows_dev // TILES_PAIR * PLANE
    dma = pltpu.SemaphoreType.DMA
    return pl.pallas_call(
        kernel,
        out_shape=jax.ShapeDtypeStruct((rows_dev // TILES_PAIR, NA * NB), BF16),
        in_specs=[pl.BlockSpec(memory_space=pl.ANY)] * 4,
        out_specs=pl.BlockSpec(memory_space=pltpu.VMEM),
        scratch_shapes=[
            pltpu.VMEM((NC * NA, depth), BF16),
            pltpu.VMEM((NC * NA, depth), BF16),
            pltpu.VMEM((B_CORE, depth, ND), BF16),
            pltpu.VMEM((B_CORE, depth, ND), BF16),
            pltpu.VMEM((PLANE, rows_dev + 16, ND), BF16),
            *[pltpu.VMEM((SLICES, 2, ROWS, WIDE), BF16)] * 6,
            *[pltpu.VMEM((SLICES, 2, ROWS, WIDE), F32)] * 2,
            *[pltpu.VMEM((SLICES, ROWS, WIDE), BF16)] * 2,
            pltpu.VMEM((OUT_ROWS, 2 * K_HALF), F32),
            pltpu.VMEM((SLICES, RING, CORES, 2, OUT_ROWS, K_HALF), BF16),
            pltpu.VMEM((2 * RING, pairs, K_HALF), BF16),
            pltpu.VMEM((SLICES, RING, 2 * OUT_ROWS, STEP), F32),
            pltpu.VMEM((SLICES, PLANE, OUT_ROWS, 128), BF16),
            pltpu.VMEM((SLICES, PLANE, OUT_ROWS, 128), BF16),
            pltpu.VMEM((16, 128), F32),
            pltpu.VMEM((NB * A_HALF, 128), F32),
            dma((4,)),
            dma((2,)), dma((2,)),
            dma((2,)), dma((2,)), dma((2,)), dma((2,)),
            dma((2, RING)), dma((2, RING)), dma((RING,)), dma((RING,)),
            dma((2, 2)), dma((2, 2)), dma((2, 2)), dma((2, 2)), dma((2, 2)), dma((2, 2)),
            dma((2,)), dma((2,)),
            dma((2, 2)), dma((2, 2)), dma((2, 2)), dma((2, 2)),
            dma((2, 5)), dma((2, 5)),
            dma((2, PLANE)), dma((2, PLANE)),
        ],
        compiler_params=pltpu.CompilerParams(
            collective_id=0, has_side_effects=True, vmem_limit_bytes=56 * 1024 * 1024
        ),
        cost_estimate=pl.CostEstimate(flops=7 * 10**9, bytes_accessed=4 * 10**6, transcendentals=0),
        name="ladder",
    )(tiles, labels, fit_a, fit_b)


def solution(mesh):
    placed = (
        P(("blk", "occ"), None),
        P(("blk", "occ"), None),
        P(("blk", "occ")),
        P(None, None, "occ"),
        P("blk", None, "occ"),
    )
    return jax.shard_map(
        on_device, mesh=mesh, in_specs=placed, out_specs=P(("blk", "occ"), None), check_vma=False
    )
```

```python
import jax
import jax.numpy as jnp
from jax import lax
from jax.experimental import pallas as pl
from jax.experimental.pallas import tpu as pltpu
from jax.sharding import PartitionSpec as P

MESH = pl.DeviceIdType.MESH
RING = 4
CORES = 2
SLICES = 2
TILES_PAIR = 16
NA, NB, NC, ND = 40, 128, 32, 128
BLOCKS_OWNER = 2
PLANE = RING * RING
A_HALF = NA // 2
C_PART = NC // RING
ROWS = C_PART * NA
B_CORE = 8
WIDE = 2 * ND
K_HALF = C_PART * ND // 2
OUT_ROWS = 2 * NA
STEP = 256

F32, BF16 = jnp.float32, jnp.bfloat16


def product(left, right, right_axis):
    return lax.dot_general(left, right, (((1,), (right_axis,)), ((), ())), preferred_element_type=F32)


def kernel(
    tiles, owner, sub_block, fit_a, fit_b, out,
    a_own, a_mate, b_own, b_mate, slots, far_out, side_out, comb_out, far_in, side_in, comb_in,
    keep_comb, keep_own, x_out, x_in, arranged, ints, summed, total, parcels, got, owners, subs, row_ids, names, final,
    load_sem, mate_s, mate_r, ring1_s, ring1_r, half1_s, half1_r, ring2_s, ring2_r, pass2_s, pass2_r,
    far_s, far_r, side_s, side_r, comb_s, comb_r, x_s, x_r, ag_s, ag_r, fw_s, fw_r, cx_s, cx_r, out_s, out_r,
):
    blk, occ = lax.axis_index("blk"), lax.axis_index("occ")
    x_hi, y = lax.div(blk, RING), lax.rem(blk, RING)
    z, x_lo, k = lax.div(occ, 4), lax.rem(lax.div(occ, 2), 2), lax.rem(occ, 2)
    x = x_hi * 2 + x_lo
    rows_dev = tiles.shape[0]
    pairs_dev = rows_dev // TILES_PAIR

    def mod(value):
        return lax.rem(value, RING)

    def device(x_at, y_at, z_at, k_at):
        return (lax.div(x_at, 2) * RING + y_at, z_at * 4 + lax.rem(x_at, 2) * 2 + k_at)

    up, down, far = mod(z + 1), mod(z + 3), mod(z + 2)
    mate = device(x, y, z, 1 - k)
    partner = device(x_hi * 2 + 1 - x_lo, y, z, k)

    def along(d):
        return device(x, y, mod(z + 1 + 2 * d), k)

    me = x * RING + y
    u, v = (1 - k) * x + k * y, (1 - k) * y + k * x

    def slot_of(u_at, v_at):
        return ((1 - k) * u_at + k * v_at) * RING + (1 - k) * v_at + k * u_at

    def plane_device(u_at, v_at):
        return device((1 - k) * u_at + k * v_at, (1 - k) * v_at + k * u_at, z, k)

    def remote(src, dst, send, recv, to):
        return pltpu.make_async_remote_copy(
            src_ref=src, dst_ref=dst, send_sem=send, recv_sem=recv, device_id=to, device_id_type=MESH
        )

    def arrival(dst, send, recv):
        remote(dst, dst, send, recv, mate).wait_recv()

    load_a = pltpu.make_async_copy(fit_a, a_own, load_sem.at[0])
    load_b = pltpu.make_async_copy(fit_b.at[pl.ds(k * B_CORE, B_CORE)], b_own, load_sem.at[1])
    load_t = pltpu.make_async_copy(tiles, slots.at[me, pl.ds(0, rows_dev)], load_sem.at[2])
    load_o = pltpu.make_async_copy(owner, owners, load_sem.at[3])
    load_u = pltpu.make_async_copy(sub_block, subs, load_sem.at[4])
    for load in (load_o, load_u, load_t, load_a, load_b):
        load.start()

    load_o.wait()
    load_u.wait()
    spot = (owners[...] * BLOCKS_OWNER + subs[...]) * 8 + lax.div(
        lax.broadcasted_iota(jnp.int32, owners.shape, 1), TILES_PAIR
    )
    slots[me, rows_dev : rows_dev + 16, :] = jnp.concatenate([spot, spot], axis=0).astype(F32).astype(BF16)
    row_ids[...] = lax.broadcasted_iota(jnp.int32, row_ids.shape, 0).astype(F32).astype(BF16)

    barrier = pltpu.get_barrier_semaphore()

    def greet(i, carry):
        to = device(mod(x + lax.div(i, RING)), mod(y + lax.rem(i, RING)), z, k)
        pl.semaphore_signal(barrier, inc=1, device_id=to, device_id_type=MESH)
        return carry

    for to in (mate, along(0), along(1)):
        pl.semaphore_signal(barrier, inc=1, device_id=to, device_id_type=MESH)
    lax.fori_loop(1, PLANE, greet, 0)
    pl.semaphore_wait(barrier, PLANE + 2)

    def swap_a(i):
        rows = pl.ds(pl.multiple_of(mod(z + (2, 1, 3, 0)[i]) * ROWS, ROWS), ROWS)
        return remote(fit_a.at[rows], a_mate.at[rows], mate_s.at[i], mate_r.at[i], mate)

    def swap_b(s):
        here, there = pl.ds((1 - k) * B_CORE + s * 4, 4), pl.ds(s * 4, 4)
        return remote(fit_b.at[here], b_mate.at[there], mate_s.at[4 + s], mate_r.at[4 + s], mate)

    swap_b(0).start()
    swap_a(0).start()

    def ring1(d):
        return remote(slots.at[me], slots.at[me], ring1_s.at[d], ring1_r.at[d], plane_device(mod(u + 1 + 2 * d), v))

    def part1(d, slot):
        start, size = (0, rows_dev // 2) if d == 0 else (rows_dev // 2, rows_dev // 2 + 16)
        return slots.at[slot, pl.ds(start, size)]

    def half1(d, back):
        ref = part1(d, slot_of(mod(u + back), v))
        return remote(ref, ref, half1_s.at[d], half1_r.at[d], plane_device(mod(u + 1 + 2 * d), v))

    def ring2(d, i):
        ref = slots.at[slot_of(mod(u + i), v)]
        return remote(ref, ref, ring2_s.at[d, i], ring2_r.at[d, i], plane_device(u, mod(v + 1 + 2 * d)))

    def pass2(i):
        d = i // 2
        ref = slots.at[slot_of(mod(u + i), mod(v + 3 - 2 * d))]
        return remote(ref, ref, pass2_s.at[i], pass2_r.at[i], plane_device(u, mod(v + 1 + 2 * d)))

    load_t.wait()
    ring1(0).start()
    ring1(1).start()
    load_a.wait()
    load_b.wait()

    def partial(part, h, s):
        rows = pl.ds(pl.multiple_of(part * ROWS, ROWS), ROWS)
        b = s * 4 + h * 2
        own = product(a_own[rows, :], jnp.concatenate([b_own[b], b_own[b + 1]], axis=1), 0)
        return own + product(a_mate[rows, :], jnp.concatenate([b_mate[b], b_mate[b + 1]], axis=1), 0)

    def far_copy(s, d):
        return remote(far_out.at[s, d], far_in.at[s, d], far_s.at[s, d], far_r.at[s, d], along(d))

    def side_copy(s, d):
        return remote(side_out.at[s, d], side_in.at[s, d], side_s.at[s, d], side_r.at[s, d], along(d))

    def comb_copy(s, d):
        return remote(comb_out.at[s, d], comb_in.at[s, d], comb_s.at[s, d], comb_r.at[s, d], along(d))

    def x_copy(s):
        return remote(x_out.at[s], x_in.at[s], x_s.at[s], x_r.at[s], partner)

    def far_piece(s, d):
        far_out[s, d] = partial(far, d, s).astype(BF16)

    def side_piece(s, d):
        side_out[s, d] = partial(mod(z + 1 + 2 * d), 1 - d, s).astype(BF16)

    def comb_piece(s, d):
        keep_comb[s, d] = partial(mod(z + 1 + 2 * d), d, s)

    def own_piece(s, d):
        keep_own[s, d] = partial(z, d, s)

    def each_way(s, piece, copy):
        def one(d, carry):
            piece(s, d)
            if copy is not None:
                copy(s, d).start()
            return carry

        lax.fori_loop(0, 2, one, 0)

    def send_comb(s):
        for d in (0, 1):
            far_copy(s, d).wait_recv()
            comb_out[s, d] = (keep_comb[s, d] + far_in[s, d].astype(F32)).astype(BF16)
            comb_copy(s, d).start()

    def build(slot):
        names[...] = slots[slot, pl.ds(rows_dev, 16), :].astype(F32)
        none = jnp.zeros((128, ND), BF16)

        def chosen(row):
            line = jnp.broadcast_to(names[row : row + 1, :], (16, 128)).astype(BF16)
            return jnp.where(row_ids[...] == jnp.concatenate([line] * 16, axis=0), 1.0, 0.0).astype(BF16)

        for j in range(rows_dev // STEP):
            choice = jnp.concatenate([chosen(2 * j), chosen(2 * j + 1)], axis=1)
            first = slots[slot, j * STEP : j * STEP + 128, :]
            second = slots[slot, j * STEP + 128 : (j + 1) * STEP, :]
            values = jnp.concatenate(
                [jnp.concatenate([first, none], axis=1), jnp.concatenate([none, second], axis=1)], axis=0
            )
            sums = product(choice, values, 0)
            rows = pl.ds(pl.multiple_of(slot * pairs_dev + j * 16, 16), 16)
            for c in range(NC):
                part = sums[c * 8 : (c + 1) * 8]
                part = jnp.concatenate([part[:, :ND], part[:, ND:]], axis=0)
                summed[c // 4, rows, (c % 4) * ND : (c % 4 + 1) * ND] = part.astype(BF16)

    def build_line(v_at):
        def one(i, carry):
            build(slot_of(i, v_at))
            return carry

        lax.fori_loop(0, RING, one, 0)

    def send_x(s):
        comb_copy(s, 0).wait_recv()
        comb_copy(s, 1).wait_recv()
        side_copy(s, 0).wait_recv()
        side_copy(s, 1).wait_recv()
        h = 1 - x_lo
        x_out[s] = (keep_own[s, h] + comb_in[s, h].astype(F32) + side_in[s, 1 - h].astype(F32)).astype(BF16)
        x_copy(s).start()

    def ag_copy(s, d):
        ref = ints.at[s, z, k]
        return remote(ref, ref, ag_s.at[s, d], ag_r.at[s, d], along(d))

    def fw_copy(s, d):
        ref = ints.at[s, mod(z + 3 - 2 * d), k, d]
        return remote(ref, ref, fw_s.at[s, d], fw_r.at[s, d], along(d))

    def cx_ref(s, i, core):
        if i < 3:
            return ints.at[s, (z, down, up)[i], core]
        return ints.at[s, far, core, i - 3]

    def cx_copy(s, i):
        ref = cx_ref(s, i, k)
        return remote(ref, ref, cx_s.at[s, i], cx_r.at[s, i], mate)

    def finish(s):
        x_copy(s).wait_recv()
        h = x_lo
        for two in range(C_PART // 2):
            rows = pl.ds(two * 2 * NA, 2 * NA)
            value = (
                keep_own[s, h, rows, :]
                + comb_in[s, h, rows, :].astype(F32)
                + side_in[s, 1 - h, rows, :].astype(F32)
                + x_in[s, rows, :].astype(F32)
            )
            for one in range(2):
                columns = pl.ds((two * 2 + one) * ND, ND)
                for b in range(2):
                    block = value[one * NA : (one + 1) * NA, b * ND : (b + 1) * ND]
                    arranged[pl.ds(b * A_HALF, A_HALF), columns] = block[:A_HALF]
                    arranged[pl.ds(NA + b * A_HALF, A_HALF), columns] = block[A_HALF:]
        for half in range(2):
            ints[s, z, k, half] = arranged[:, half * K_HALF : (half + 1) * K_HALF].astype(BF16)
        ag_copy(s, 0).start()
        ag_copy(s, 1).start()
        cx_copy(s, 0).start()

    def forward(s):
        for d in (0, 1):
            from_z = mod(z + 3 - 2 * d)
            arrival(ints.at[s, from_z, k], ag_s.at[s, d], ag_r.at[s, d])
            fw_copy(s, d).start()
            cx_copy(s, 1 + d).start()

    def last_forward(s):
        for d in (0, 1):
            arrival(ints.at[s, far, k, d], fw_s.at[s, d], fw_r.at[s, d])
            cx_copy(s, 3 + d).start()

    def multiply(s, part, halves, first):
        left = [jnp.concatenate([ints[s, part, 0, i], ints[s, part, 1, i]], axis=0) for i in halves]

        def one(n, carry):
            rows = pl.ds(pl.multiple_of(n * 512, 512), 512)
            value = sum(product(summed[part * 2 + i, rows, :], left[at], 1) for at, i in enumerate(halves))
            total[s, rows, : 2 * OUT_ROWS] = value if first else total[s, rows, : 2 * OUT_ROWS] + value
            return carry

        lax.fori_loop(0, total.shape[1] // 512, one, 0)

    def gathered(s, i):
        arrival(cx_ref(s, i, 1 - k), cx_s.at[s, i], cx_r.at[s, i])
        if i < 3:
            multiply(s, (z, down, up)[i], (0, 1), i == 0)
        else:
            multiply(s, far, (i - 3,), False)

    def out_copy(s, i):
        x_at, y_at = mod(x + lax.div(i, RING)), mod(y + lax.rem(i, RING))
        return remote(
            parcels.at[s, x_at * RING + y_at], got.at[s, me], out_s.at[s, i], out_r.at[s, i], device(x_at, y_at, z, k)
        )

    def send_out(s):
        low = lax.broadcasted_iota(jnp.int32, (OUT_ROWS, 128), 1) < 64

        def pack(n, carry):
            rows = pl.ds(pl.multiple_of(n * 128, 128), 128)
            value = jnp.concatenate([total[s, rows, :128].T, total[s, rows, 128:].T[: 2 * OUT_ROWS - 128]], axis=0)
            top = jnp.concatenate([value[0:NA], value[2 * NA : 3 * NA]], axis=0)
            bottom = jnp.concatenate([value[NA : 2 * NA], value[3 * NA : 4 * NA]], axis=0)
            parcels[s, 2 * n] = jnp.where(low, top, pltpu.roll(bottom, 64, 1)).astype(BF16)
            parcels[s, 2 * n + 1] = jnp.where(low, pltpu.roll(top, 64, 1), bottom).astype(BF16)
            return carry

        def send(i, carry):
            out_copy(s, i).start()
            return carry

        lax.fori_loop(0, PLANE // 2, pack, 0)
        lax.fori_loop(1, PLANE, send, 0)

    def unpack(s, x_at, y_at, value):
        base = (lax.div(x_at, 2) * RING + y_at) * 16 + s * 4 + lax.rem(x_at, 2) * 2
        for core in range(CORES):
            rows = pl.ds(pl.multiple_of((base + core * 8) * A_HALF, 8), NA)
            final[rows, :] = value[core * NA : (core + 1) * NA]

    def receive(s):
        unpack(s, x, y, parcels[s, me].astype(F32))

        def one(i, carry):
            x_at, y_at = mod(x + RING - lax.div(i, RING)), mod(y + RING - lax.rem(i, RING))
            slot = x_at * RING + y_at
            arrival(got.at[s, slot], out_s.at[s, i], out_r.at[s, i])
            unpack(s, x_at, y_at, got[s, slot].astype(F32))
            return carry

        lax.fori_loop(1, PLANE, one, 0)

    swap_a(0).wait_recv()
    swap_b(0).wait_recv()
    for i in (1, 2):
        swap_a(i).start()
    each_way(0, far_piece, far_copy)
    swap_b(1).start()
    swap_a(3).start()
    swap_a(1).wait_recv()
    swap_a(2).wait_recv()
    each_way(0, side_piece, side_copy)
    each_way(0, comb_piece, None)
    arrival(slots.at[slot_of(mod(u + 3), v)], ring1_s.at[0], ring1_r.at[0])
    half1(0, 3).start()
    arrival(slots.at[slot_of(mod(u + 1), v)], ring1_s.at[1], ring1_r.at[1])
    half1(1, 1).start()
    for i in (0, 1, 3):
        for d in (0, 1):
            ring2(d, i).start()
    swap_b(1).wait_recv()
    swap_a(3).wait_recv()
    each_way(1, far_piece, None)
    each_way(1, side_piece, None)
    each_way(1, comb_piece, None)
    send_comb(0)
    for d in (0, 1):
        far_copy(1, d).start()
    for d in (0, 1):
        arrival(part1(d, slot_of(mod(u + 2), v)), half1_s.at[d], half1_r.at[d])
    for d in (0, 1):
        ring2(d, 2).start()
    each_way(0, own_piece, None)
    each_way(1, own_piece, None)
    build_line(v)
    send_x(0)
    send_comb(1)
    for d in (0, 1):
        side_copy(1, d).start()
    for i in range(RING):
        arrival(slots.at[slot_of(mod(u + i), mod(v + 3))], ring2_s.at[0, i], ring2_r.at[0, i])
        if i < 2:
            pass2(i).start()
    for i in range(RING):
        arrival(slots.at[slot_of(mod(u + i), mod(v + 1))], ring2_s.at[1, i], ring2_r.at[1, i])
        if i >= 2:
            pass2(i).start()
    build_line(mod(v + 3))
    finish(0)
    build_line(mod(v + 1))
    send_x(1)
    forward(0)
    for i in range(RING):
        arrival(slots.at[slot_of(mod(u + i), mod(v + 2))], pass2_s.at[i], pass2_r.at[i])
    build_line(mod(v + 2))
    finish(1)
    for i in range(3):
        gathered(0, i)
    last_forward(0)
    for i in range(3, 5):
        gathered(0, i)
    send_out(0)
    forward(1)
    for i in range(3):
        gathered(1, i)
    last_forward(1)
    receive(0)
    for i in range(3, 5):
        gathered(1, i)
    send_out(1)
    receive(1)
    for i in range(A_HALF):
        value = final[pl.ds(i, NB, stride=A_HALF), :]
        turned = value.T.astype(BF16)
        out[:, i * NB : (i + 1) * NB] = turned[:pairs_dev]
        out[:, (i + A_HALF) * NB : (i + A_HALF + 1) * NB] = turned[pairs_dev:]

    for i in range(RING):
        swap_a(i).wait_send()
    for s in range(SLICES):
        swap_b(s).wait_send()
    for d in (0, 1):
        ring1(d).wait_send()
        half1(d, 3 - 2 * d).wait_send()
        for i in range(RING):
            ring2(d, i).wait_send()
    for i in range(RING):
        pass2(i).wait_send()
    for s in range(SLICES):
        x_copy(s).wait_send()
        for d in (0, 1):
            far_copy(s, d).wait_send()
            side_copy(s, d).wait_send()
            comb_copy(s, d).wait_send()
            ag_copy(s, d).wait_send()
            fw_copy(s, d).wait_send()
        for i in range(5):
            cx_copy(s, i).wait_send()

        def sent(i, carry):
            out_copy(s, i).wait_send()
            return carry

        lax.fori_loop(1, PLANE, sent, 0)


def on_device(tiles, owner, sub_block, fit_ac, fit_bd):
    rows_dev = tiles.shape[0]
    depth = fit_ac.shape[2]
    owner = owner.reshape(rows_dev // 128, 128)
    sub_block = sub_block.reshape(rows_dev // 128, 128)
    fit_a = fit_ac.reshape(NC * NA, depth)
    fit_b = jnp.swapaxes(fit_bd, 1, 2)
    pairs = rows_dev // TILES_PAIR * PLANE
    dma = pltpu.SemaphoreType.DMA
    return pl.pallas_call(
        kernel,
        out_shape=jax.ShapeDtypeStruct((rows_dev // TILES_PAIR, NA * NB), BF16),
        in_specs=[pl.BlockSpec(memory_space=pl.ANY)] * 5,
        out_specs=pl.BlockSpec(memory_space=pltpu.VMEM),
        scratch_shapes=[
            pltpu.VMEM((NC * NA, depth), BF16),
            pltpu.VMEM((NC * NA, depth), BF16),
            pltpu.VMEM((B_CORE, depth, ND), BF16),
            pltpu.VMEM((B_CORE, depth, ND), BF16),
            pltpu.VMEM((PLANE, rows_dev + 16, ND), BF16),
            *[pltpu.VMEM((SLICES, 2, ROWS, WIDE), BF16)] * 6,
            *[pltpu.VMEM((SLICES, 2, ROWS, WIDE), F32)] * 2,
            *[pltpu.VMEM((SLICES, ROWS, WIDE), BF16)] * 2,
            pltpu.VMEM((OUT_ROWS, 2 * K_HALF), F32),
            pltpu.VMEM((SLICES, RING, CORES, 2, OUT_ROWS, K_HALF), BF16),
            pltpu.VMEM((2 * RING, pairs, K_HALF), BF16),
            pltpu.VMEM((SLICES, pairs, STEP), F32),
            pltpu.VMEM((SLICES, PLANE, OUT_ROWS, 128), BF16),
            pltpu.VMEM((SLICES, PLANE, OUT_ROWS, 128), BF16),
            *[pltpu.VMEM((rows_dev // 128, 128), jnp.int32)] * 2,
            pltpu.VMEM((STEP, 128), BF16),
            pltpu.VMEM((16, 128), F32),
            pltpu.VMEM((NB * A_HALF, 128), F32),
            dma((5,)),
            dma((6,)), dma((6,)),
            dma((2,)), dma((2,)), dma((2,)), dma((2,)),
            dma((2, RING)), dma((2, RING)), dma((RING,)), dma((RING,)),
            dma((2, 2)), dma((2, 2)), dma((2, 2)), dma((2, 2)), dma((2, 2)), dma((2, 2)),
            dma((2,)), dma((2,)),
            dma((2, 2)), dma((2, 2)), dma((2, 2)), dma((2, 2)),
            dma((2, 5)), dma((2, 5)),
            dma((2, PLANE)), dma((2, PLANE)),
        ],
        compiler_params=pltpu.CompilerParams(
            collective_id=0, has_side_effects=True, vmem_limit_bytes=56 * 1024 * 1024
        ),
        cost_estimate=pl.CostEstimate(flops=7 * 10**9, bytes_accessed=4 * 10**6, transcendentals=0),
        name="ladder",
    )(tiles, owner, sub_block, fit_a, fit_b)


def solution(mesh):
    placed = (
        P(("blk", "occ"), None),
        P(("blk", "occ"), None),
        P(("blk", "occ")),
        P(None, None, "occ"),
        P("blk", None, "occ"),
    )
    return jax.shard_map(
        on_device, mesh=mesh, in_specs=placed, out_specs=P(("blk", "occ"), None), check_vma=False
    )
```

```python
import jax
import jax.numpy as jnp
from jax import lax
from jax.experimental import pallas as pl
from jax.experimental.pallas import tpu as pltpu
from jax.sharding import PartitionSpec as P

MESH = pl.DeviceIdType.MESH
RING = 4
CORES = 2
SLICES = 4
GROUPS = 2
TILES_PAIR = 16
NA, NB, NC, ND = 40, 128, 32, 128
BLOCKS_OWNER = 2
PLANE = RING * RING
A_HALF = NA // 2
PART = 640
C_PART = NC // RING
ROWS = C_PART * NA
B_CORE = 8
X_PARTS = 1
X_ROWS = ROWS // X_PARTS
K_HALF = C_PART * ND // 2
OUT_ROWS = 2 * CORES * A_HALF
B_STRIDE = 24
STEP = 256

F32, BF16 = jnp.float32, jnp.bfloat16


def product(left, right, right_axis):
    return lax.dot_general(left, right, (((1,), (right_axis,)), ((), ())), preferred_element_type=F32)


def kernel(
    tiles, owner, sub_block, fit_a, fit_b, out,
    a_own, a_mate, b_own, b_mate, slots, far_out, side_out, comb_out, far_in, side_in, comb_in,
    keep_comb, keep_own, x_out, x_in, ints, summed, total, parcels, got, owners, subs, row_ids, names, final,
    load_sem, mate_s, mate_r, ring1_s, ring1_r, half1_s, half1_r, ring2_s, ring2_r, pass2_s, pass2_r,
    far_s, far_r, side_s, side_r, comb_s, comb_r, x_s, x_r, ag_s, ag_r, fw_s, fw_r, cx_s, cx_r, out_s, out_r,
):
    blk, occ = lax.axis_index("blk"), lax.axis_index("occ")
    x_hi, y = lax.div(blk, RING), lax.rem(blk, RING)
    z, x_lo, k = lax.div(occ, 4), lax.rem(lax.div(occ, 2), 2), lax.rem(occ, 2)
    x = x_hi * 2 + x_lo
    rows_dev = tiles.shape[0]
    pairs_dev = rows_dev // TILES_PAIR

    def mod(value):
        return lax.rem(value, RING)

    def device(x_at, y_at, z_at, k_at):
        return (lax.div(x_at, 2) * RING + y_at, z_at * 4 + lax.rem(x_at, 2) * 2 + k_at)

    up, down, far = mod(z + 1), mod(z + 3), mod(z + 2)
    mate = device(x, y, z, 1 - k)
    partner = device(x_hi * 2 + 1 - x_lo, y, z, k)

    def along(d):
        return device(x, y, mod(z + 1 + 2 * d), k)

    me = x * RING + y
    def cross(g, u_at, v_at):
        return (u_at, v_at) if g == 0 else (v_at, u_at)

    uv = (cross(0, x, y), cross(1, x, y))

    sizes = (PART, rows_dev + 16 - PART)

    def part_of(g, back_u, back_v, start=0, size=None):
        x_at, y_at = cross(g, mod(uv[g][0] + back_u), mod(uv[g][1] + back_v))
        return slots.at[x_at * RING + y_at, pl.ds(g * PART + start, sizes[g] if size is None else size)]

    def plane_device(g, ahead_u, ahead_v):
        return device(*cross(g, mod(uv[g][0] + ahead_u), mod(uv[g][1] + ahead_v)), z, k)

    def remote(src, dst, send, recv, to):
        return pltpu.make_async_remote_copy(
            src_ref=src, dst_ref=dst, send_sem=send, recv_sem=recv, device_id=to, device_id_type=MESH
        )

    def arrival(dst, send, recv):
        remote(dst, dst, send, recv, mate).wait_recv()

    load_a = pltpu.make_async_copy(fit_a, a_own, load_sem.at[0])
    load_b = pltpu.make_async_copy(fit_b.at[pl.ds(k * B_CORE, B_CORE)], b_own, load_sem.at[1])
    load_t = pltpu.make_async_copy(tiles, slots.at[me, pl.ds(0, rows_dev)], load_sem.at[2])
    load_o = pltpu.make_async_copy(owner, owners, load_sem.at[3])
    load_u = pltpu.make_async_copy(sub_block, subs, load_sem.at[4])
    for load in (load_o, load_u, load_t, load_a, load_b):
        load.start()

    load_o.wait()
    load_u.wait()
    spot = (owners[...] * BLOCKS_OWNER + subs[...]) * 8 + lax.div(
        lax.broadcasted_iota(jnp.int32, owners.shape, 1), TILES_PAIR
    )
    slots[me, rows_dev : rows_dev + 16, :] = jnp.concatenate([spot, spot], axis=0).astype(F32).astype(BF16)
    row_ids[...] = lax.broadcasted_iota(jnp.int32, row_ids.shape, 0).astype(F32).astype(BF16)

    barrier = pltpu.get_barrier_semaphore()

    def greet(i, carry):
        to = device(mod(x + lax.div(i, RING)), mod(y + lax.rem(i, RING)), z, k)
        pl.semaphore_signal(barrier, inc=1, device_id=to, device_id_type=MESH)
        return carry

    for to in (mate, along(0), along(1)):
        pl.semaphore_signal(barrier, inc=1, device_id=to, device_id_type=MESH)
    lax.fori_loop(1, PLANE, greet, 0)
    pl.semaphore_wait(barrier, PLANE + 2)

    def swap_a(i):
        rows = pl.ds(pl.multiple_of(mod(z + (2, 1, 3, 0)[i]) * ROWS, ROWS), ROWS)
        return remote(fit_a.at[rows], a_mate.at[rows], mate_s.at[i], mate_r.at[i], mate)

    def swap_b(t):
        here, there = pl.ds((1 - k) * B_CORE + t * 4, 4), pl.ds(t * 4, 4)
        return remote(fit_b.at[here], b_mate.at[there], mate_s.at[4 + t], mate_r.at[4 + t], mate)

    swap_b(0).start()
    swap_a(0).start()

    def ring1(g, d):
        ref = part_of(g, 0, 0)
        return remote(ref, ref, ring1_s.at[g, d], ring1_r.at[g, d], plane_device(g, 1 + 2 * d, 0))

    def half_ref(g, d, back):
        first = sizes[g] // 32 * 16
        return part_of(g, back, 0, d * first, sizes[g] - first if d else first)

    def half1(g, d):
        ref = half_ref(g, d, 3 - 2 * d)
        return remote(ref, ref, half1_s.at[g, d], half1_r.at[g, d], plane_device(g, 1 + 2 * d, 0))

    def ring2(g, d, i):
        ref = part_of(g, i, 0)
        return remote(ref, ref, ring2_s.at[g, d, i], ring2_r.at[g, d, i], plane_device(g, 0, 1 + 2 * d))

    def pass2(g, i):
        d = i // 2
        ref = part_of(g, i, 3 - 2 * d)
        return remote(ref, ref, pass2_s.at[g, i], pass2_r.at[g, i], plane_device(g, 0, 1 + 2 * d))

    def both_ways(i):
        for g in range(2):
            for d in (0, 1):
                ring2(g, d, i).start()

    def pass_on(d, i):
        for g in range(2):
            arrival(part_of(g, i, 3 - 2 * d), ring2_s.at[g, d, i], ring2_r.at[g, d, i])
            if i // 2 == d:
                pass2(g, i).start()

    load_t.wait()
    for g in range(2):
        for d in (0, 1):
            ring1(g, d).start()
    both_ways(0)
    load_a.wait()
    load_b.wait()

    def partial(part, h, t):
        rows = pl.ds(pl.multiple_of(part * ROWS, ROWS), ROWS)
        b = t * 4 + h * 2
        own = product(a_own[rows, :], jnp.concatenate([b_own[b], b_own[b + 1]], axis=1), 0)
        return own + product(a_mate[rows, :], jnp.concatenate([b_mate[b], b_mate[b + 1]], axis=1), 0)

    def far_copy(s, d):
        return remote(far_out.at[s, d], far_in.at[s, d], far_s.at[s, d], far_r.at[s, d], along(d))

    def side_copy(s, d):
        return remote(side_out.at[s, d], side_in.at[s, d], side_s.at[s, d], side_r.at[s, d], along(d))

    def comb_copy(s, d):
        return remote(comb_out.at[s, d], comb_in.at[s, d], comb_s.at[s, d], comb_r.at[s, d], along(d))

    def x_copy(s, i):
        rows = pl.ds(i * X_ROWS, X_ROWS)
        return remote(x_out.at[s, rows], x_in.at[s, rows], x_s.at[s, i], x_r.at[s, i], partner)

    def keep(ref, t, d, value):
        ref[2 * t, d] = value[:, :ND].astype(ref.dtype)
        ref[2 * t + 1, d] = value[:, ND:].astype(ref.dtype)

    def far_piece(t, d):
        keep(far_out, t, d, partial(far, d, t))

    def side_piece(t, d):
        keep(side_out, t, d, partial(mod(z + 1 + 2 * d), 1 - d, t))

    def comb_piece(t, d):
        keep(keep_comb, t, d, partial(mod(z + 1 + 2 * d), d, t))

    def own_piece(t, d):
        keep(keep_own, t, d, partial(z, d, t))

    def each_way(t, piece):
        def one(d, carry):
            piece(t, d)
            return carry

        lax.fori_loop(0, 2, one, 0)

    def both(s, copy):
        copy(s, 0).start()
        copy(s, 1).start()

    def send_comb(s):
        for d in (0, 1):
            far_copy(s, d).wait_recv()
            comb_out[s, d] = (keep_comb[s, d] + far_in[s, d].astype(F32)).astype(BF16)
            comb_copy(s, d).start()

    def build(slot):
        names[...] = slots[slot, pl.ds(rows_dev, 16), :].astype(F32)
        none = jnp.zeros((128, ND), BF16)

        def chosen(row):
            line = jnp.broadcast_to(names[row : row + 1, :], (16, 128)).astype(BF16)
            return jnp.where(row_ids[...] == jnp.concatenate([line] * 16, axis=0), 1.0, 0.0).astype(BF16)

        for j in range(rows_dev // STEP):
            choice = jnp.concatenate([chosen(2 * j), chosen(2 * j + 1)], axis=1)
            first = slots[slot, j * STEP : j * STEP + 128, :]
            second = slots[slot, j * STEP + 128 : (j + 1) * STEP, :]
            values = jnp.concatenate(
                [jnp.concatenate([first, none], axis=1), jnp.concatenate([none, second], axis=1)], axis=0
            )
            sums = product(choice, values, 0)
            rows = pl.ds(pl.multiple_of(slot * pairs_dev + j * 16, 16), 16)
            for c in range(NC):
                part = sums[c * 8 : (c + 1) * 8]
                part = jnp.concatenate([part[:, :ND], part[:, ND:]], axis=0)
                summed[c // 4, rows, (c % 4) * ND : (c % 4 + 1) * ND] = part.astype(BF16)

    def build_near(dx, first, last):
        def one(i, carry):
            build(mod(x + dx) * RING + mod(y + i + i // 2))
            return carry

        lax.fori_loop(first, last, one, 0)

    def build_far(first, last):
        def one(i, carry):
            build(mod(x + 2) * RING + mod(y + i))
            return carry

        lax.fori_loop(first, last, one, 0)

    def send_x(s):
        comb_copy(s, 0).wait_recv()
        comb_copy(s, 1).wait_recv()
        side_copy(s, 0).wait_recv()
        side_copy(s, 1).wait_recv()
        h = 1 - x_lo
        x_out[s] = (keep_own[s, h] + comb_in[s, h].astype(F32) + side_in[s, 1 - h].astype(F32)).astype(BF16)
        for i in range(X_PARTS):
            x_copy(s, i).start()

    def ag_copy(s, d):
        ref = ints.at[s, z, k]
        return remote(ref, ref, ag_s.at[s, d], ag_r.at[s, d], along(d))

    def fw_ref(s, part, core, d):
        return ints.at[s, part, core, :, pl.ds(d * STEP, STEP)]

    def fw_copy(s, d):
        ref = fw_ref(s, mod(z + 3 - 2 * d), k, d)
        return remote(ref, ref, fw_s.at[s, d], fw_r.at[s, d], along(d))

    def cx_ref(s, i, core):
        if i < 3:
            return ints.at[s, (z, down, up)[i], core]
        return fw_ref(s, far, core, i - 3)

    def cx_copy(s, i):
        ref = cx_ref(s, i, k)
        return remote(ref, ref, cx_s.at[s, i], cx_r.at[s, i], mate)

    def finish(s):
        for i in range(X_PARTS):
            x_copy(s, i).wait_recv()
        h = x_lo
        blocks = []
        for two in range(C_PART // 2):
            rows = pl.ds(two * 2 * NA, 2 * NA)
            value = (
                keep_own[s, h, rows, :]
                + comb_in[s, h, rows, :].astype(F32)
                + side_in[s, 1 - h, rows, :].astype(F32)
                + x_in[s, rows, :].astype(F32)
            )
            blocks += [value[:NA], value[NA:]]
        lines = [jnp.concatenate(blocks[i * 4 : i * 4 + 4], axis=1) for i in range(2)]
        ints[s, z, k] = jnp.concatenate(lines, axis=0).astype(BF16)
        ag_copy(s, 0).start()
        ag_copy(s, 1).start()
        cx_copy(s, 0).start()

    def forward(s):
        for d in (0, 1):
            from_z = mod(z + 3 - 2 * d)
            arrival(ints.at[s, from_z, k], ag_s.at[s, d], ag_r.at[s, d])
            fw_copy(s, d).start()
            cx_copy(s, 1 + d).start()

    def last_forward(s):
        for d in (0, 1):
            arrival(fw_ref(s, far, k, d), fw_s.at[s, d], fw_r.at[s, d])
            cx_copy(s, 3 + d).start()

    def multiply(t, part, first):
        left = [[], []]
        for s in (2 * t, 2 * t + 1):
            for core in range(CORES):
                value = ints[s, part, core].astype(F32)
                left[0].append(value[:NA])
                left[1].append(value[NA:])
        left = [jnp.concatenate(value, axis=0).astype(BF16) for value in left]

        def one(n, carry):
            rows = pl.ds(pl.multiple_of(n * 512, 512), 512)
            value = product(summed[part * 2, rows, :], left[0], 1) + product(summed[part * 2 + 1, rows, :], left[1], 1)
            total[t, rows, : 4 * NA] = value if first else total[t, rows, : 4 * NA] + value
            return carry

        lax.fori_loop(0, total.shape[1] // 512, one, 0)

    def gathered(t, i):
        for s in (2 * t, 2 * t + 1):
            arrival(cx_ref(s, i, 1 - k), cx_s.at[s, i], cx_r.at[s, i])
            if i == 3:
                arrival(cx_ref(s, 4, 1 - k), cx_s.at[s, 4], cx_r.at[s, 4])
        multiply(t, (z, down, up, far)[i], i == 0)

    def out_copy(t, i):
        x_at, y_at = mod(x + lax.div(i, RING)), mod(y + lax.rem(i, RING))
        return remote(
            parcels.at[t, x_at * RING + y_at], got.at[t, me], out_s.at[t, i], out_r.at[t, i], device(x_at, y_at, z, k)
        )

    def send_out(t):
        low = lax.broadcasted_iota(jnp.int32, (OUT_ROWS, 128), 1) < 64
        for n in range(PLANE // 2):
            rows = slice(n * 128, (n + 1) * 128)
            value = jnp.concatenate([total[t, rows, :128].T, total[t, rows, 128:].T[: 4 * NA - 128]], axis=0)
            top = jnp.concatenate([value[i * NA : i * NA + A_HALF] for i in range(4)], axis=0)
            bottom = jnp.concatenate([value[i * NA + A_HALF : (i + 1) * NA] for i in range(4)], axis=0)
            parcels[t, 2 * n] = jnp.where(low, top, pltpu.roll(bottom, 64, 1)).astype(BF16)
            parcels[t, 2 * n + 1] = jnp.where(low, pltpu.roll(top, 64, 1), bottom).astype(BF16)

        def send(i, carry):
            out_copy(t, i).start()
            return carry

        lax.fori_loop(1, PLANE, send, 0)

    def unpack(t, x_at, y_at, value):
        base = (lax.div(x_at, 2) * RING + y_at) * 16 + t * 4 + lax.rem(x_at, 2) * 2
        for at in range(4):
            rows = pl.ds(pl.multiple_of((base + at % 2 * 8 + at // 2) * B_STRIDE, 8), A_HALF)
            final[rows, :] = value[at * A_HALF : (at + 1) * A_HALF]

    def receive(t):
        unpack(t, x, y, parcels[t, me].astype(F32))

        def one(i, carry):
            x_at, y_at = mod(x + RING - lax.div(i, RING)), mod(y + RING - lax.rem(i, RING))
            slot = x_at * RING + y_at
            arrival(got.at[t, slot], out_s.at[t, i], out_r.at[t, i])
            unpack(t, x_at, y_at, got[t, slot].astype(F32))
            return carry

        lax.fori_loop(1, PLANE, one, 0)

    swap_a(0).wait_recv()
    swap_b(0).wait_recv()
    for i in (1, 2):
        swap_a(i).start()
    for d in (0, 1):
        far_piece(0, d)
        far_copy(0, d).start()
        far_copy(1, d).start()
    swap_b(1).start()
    swap_a(3).start()
    swap_a(1).wait_recv()
    swap_a(2).wait_recv()
    each_way(0, side_piece)
    both(0, side_copy)
    each_way(0, comb_piece)
    for g in range(2):
        for d in (0, 1):
            arrival(part_of(g, 3 - 2 * d, 0), ring1_s.at[g, d], ring1_r.at[g, d])
            half1(g, d).start()
    both_ways(3)
    both_ways(1)
    swap_b(1).wait_recv()
    swap_a(3).wait_recv()
    each_way(1, far_piece)
    send_comb(0)
    both(1, side_copy)
    send_comb(1)
    both(2, far_copy)
    both(3, far_copy)
    for g in range(2):
        for d in (0, 1):
            arrival(half_ref(g, d, 2), half1_s.at[g, d], half1_r.at[g, d])
    both_ways(2)
    each_way(1, side_piece)
    both(2, side_copy)
    each_way(1, comb_piece)
    each_way(0, own_piece)
    each_way(1, own_piece)
    send_x(0)
    pass_on(0, 0)
    pass_on(1, 3)
    build_near(0, 0, 1)
    send_x(1)
    pass_on(0, 1)
    send_comb(2)
    both(3, side_copy)
    pass_on(1, 2)
    for d, i in ((0, 3), (0, 2), (1, 0), (1, 1)):
        pass_on(d, i)
    send_comb(3)
    build_near(0, 1, 3)
    finish(0)
    build_near(1, 0, 3)
    finish(1)
    send_x(2)
    build_near(3, 0, 3)
    for g in range(2):
        for i in range(RING):
            arrival(part_of(g, i, 2), pass2_s.at[g, i], pass2_r.at[g, i])
    build_far(0, RING)
    send_x(3)
    for dx in (0, 1, 3):
        build(mod(x + dx) * RING + mod(y + 2))
    finish(2)
    gathered(0, 0)
    forward(0)
    finish(3)
    forward(1)
    gathered(0, 1)
    gathered(0, 2)
    forward(2)
    last_forward(0)
    gathered(1, 0)
    forward(3)
    last_forward(1)
    gathered(0, 3)
    last_forward(2)
    send_out(0)
    last_forward(3)
    for i in (1, 2, 3):
        gathered(1, i)
    send_out(1)
    for t in range(GROUPS):
        receive(t)
    for i in range(A_HALF):
        value = final[pl.ds(i, NB, stride=B_STRIDE), :]
        turned = value.T.astype(BF16)
        out[:, i * NB : (i + 1) * NB] = turned[:pairs_dev]
        out[:, (i + A_HALF) * NB : (i + A_HALF + 1) * NB] = turned[pairs_dev:]

    for i in range(RING):
        swap_a(i).wait_send()
    for t in range(2):
        swap_b(t).wait_send()
    for g in range(2):
        for d in (0, 1):
            ring1(g, d).wait_send()
            half1(g, d).wait_send()
            for i in range(RING):
                ring2(g, d, i).wait_send()
        for i in range(RING):
            pass2(g, i).wait_send()
    for s in range(SLICES):
        for i in range(X_PARTS):
            x_copy(s, i).wait_send()
        for d in (0, 1):
            far_copy(s, d).wait_send()
            side_copy(s, d).wait_send()
            comb_copy(s, d).wait_send()
            ag_copy(s, d).wait_send()
            fw_copy(s, d).wait_send()
        for i in range(5):
            cx_copy(s, i).wait_send()

    def sent(i, carry):
        for t in range(GROUPS):
            out_copy(t, i).wait_send()
        return carry

    lax.fori_loop(1, PLANE, sent, 0)


def on_device(tiles, owner, sub_block, fit_ac, fit_bd):
    rows_dev = tiles.shape[0]
    depth = fit_ac.shape[2]
    owner = owner.reshape(rows_dev // 128, 128)
    sub_block = sub_block.reshape(rows_dev // 128, 128)
    fit_a = fit_ac.reshape(NC * NA, depth)
    fit_b = jnp.swapaxes(fit_bd, 1, 2)
    pairs = rows_dev // TILES_PAIR * PLANE
    dma = pltpu.SemaphoreType.DMA
    return pl.pallas_call(
        kernel,
        out_shape=jax.ShapeDtypeStruct((rows_dev // TILES_PAIR, NA * NB), BF16),
        in_specs=[pl.BlockSpec(memory_space=pl.ANY)] * 5,
        out_specs=pl.BlockSpec(memory_space=pltpu.VMEM),
        scratch_shapes=[
            pltpu.VMEM((NC * NA, depth), BF16),
            pltpu.VMEM((NC * NA, depth), BF16),
            pltpu.VMEM((B_CORE, depth, ND), BF16),
            pltpu.VMEM((B_CORE, depth, ND), BF16),
            pltpu.VMEM((PLANE, rows_dev + 16, ND), BF16),
            *[pltpu.VMEM((SLICES, 2, ROWS, ND), BF16)] * 6,
            *[pltpu.VMEM((SLICES, 2, ROWS, ND), F32)] * 2,
            *[pltpu.VMEM((SLICES, ROWS, ND), BF16)] * 2,
            pltpu.VMEM((SLICES, RING, CORES, 2 * NA, K_HALF), BF16),
            pltpu.VMEM((2 * RING, pairs, K_HALF), BF16),
            pltpu.VMEM((GROUPS, pairs, STEP), F32),
            *[pltpu.VMEM((GROUPS, PLANE, OUT_ROWS, 128), BF16)] * 2,
            *[pltpu.VMEM((rows_dev // 128, 128), jnp.int32)] * 2,
            pltpu.VMEM((STEP, 128), BF16),
            pltpu.VMEM((16, 128), F32),
            pltpu.VMEM((NB * B_STRIDE, 128), F32),
            dma((5,)),
            dma((6,)), dma((6,)),
            *[dma((2, 2))] * 4,
            *[dma((2, 2, RING))] * 2,
            *[dma((2, RING))] * 2,
            *[dma((SLICES, 2))] * 6,
            *[dma((SLICES, X_PARTS))] * 2,
            *[dma((SLICES, 2))] * 4,
            *[dma((SLICES, 5))] * 2,
            *[dma((GROUPS, PLANE))] * 2,
        ],
        compiler_params=pltpu.CompilerParams(
            collective_id=0, has_side_effects=True, vmem_limit_bytes=56 * 1024 * 1024
        ),
        cost_estimate=pl.CostEstimate(flops=7 * 10**9, bytes_accessed=4 * 10**6, transcendentals=0),
        name="ladder",
    )(tiles, owner, sub_block, fit_a, fit_b)


def solution(mesh):
    placed = (
        P(("blk", "occ"), None),
        P(("blk", "occ"), None),
        P(("blk", "occ")),
        P(None, None, "occ"),
        P("blk", None, "occ"),
    )
    return jax.shard_map(
        on_device, mesh=mesh, in_specs=placed, out_specs=P(("blk", "occ"), None), check_vma=False
    )
```

```python
import jax
import jax.numpy as jnp
from jax import lax
from jax.experimental import pallas as pl
from jax.experimental.pallas import tpu as pltpu
from jax.sharding import PartitionSpec as P

MESH = pl.DeviceIdType.MESH
RING = 4
CORES = 2
SLICES = 4
GROUPS = 2
TILES_PAIR = 16
NA, NB, NC, ND = 40, 128, 32, 128
BLOCKS_OWNER = 2
PLANE = RING * RING
A_HALF = NA // 2
PART = 640
C_PART = NC // RING
ROWS = C_PART * NA
B_CORE = 8
X_PARTS = 1
X_ROWS = ROWS // X_PARTS
K_HALF = C_PART * ND // 2
OUT_ROWS = 2 * CORES * A_HALF
B_STRIDE = 24
STEP = 256
FARTHEST_FIRST = (10, 9, 6, 11, 14, 8, 2, 5, 15, 7, 13, 4, 1, 12, 3)

F32, BF16 = jnp.float32, jnp.bfloat16


def product(left, right, right_axis):
    return lax.dot_general(left, right, (((1,), (right_axis,)), ((), ())), preferred_element_type=F32)


def kernel(
    tiles, owner, sub_block, fit_a, fit_b, out,
    a_own, a_mate, b_own, b_mate, slots, far_out, side_out, comb_out, far_in, side_in, comb_in,
    keep_comb, keep_own, x_out, x_in, ints, summed, total, parcels, got, owners, subs, row_ids, names, final,
    load_sem, mate_s, mate_r, ring1_s, ring1_r, half1_s, half1_r, ring2_s, ring2_r, pass2_s, pass2_r,
    far_s, far_r, side_s, side_r, comb_s, comb_r, x_s, x_r, ag_s, ag_r, fw_s, fw_r, cx_s, cx_r, out_s, out_r,
):
    blk, occ = lax.axis_index("blk"), lax.axis_index("occ")
    x_hi, y = lax.div(blk, RING), lax.rem(blk, RING)
    z, x_lo, k = lax.div(occ, 4), lax.rem(lax.div(occ, 2), 2), lax.rem(occ, 2)
    x = x_hi * 2 + x_lo
    rows_dev = tiles.shape[0]
    pairs_dev = rows_dev // TILES_PAIR

    def mod(value):
        return lax.rem(value, RING)

    def device(x_at, y_at, z_at, k_at):
        return (lax.div(x_at, 2) * RING + y_at, z_at * 4 + lax.rem(x_at, 2) * 2 + k_at)

    up, down, far = mod(z + 1), mod(z + 3), mod(z + 2)
    mate = device(x, y, z, 1 - k)
    partner = device(x_hi * 2 + 1 - x_lo, y, z, k)

    def along(d):
        return device(x, y, mod(z + 1 + 2 * d), k)

    me = x * RING + y
    def cross(g, u_at, v_at):
        return (u_at, v_at) if g == 0 else (v_at, u_at)

    uv = (cross(0, x, y), cross(1, x, y))

    sizes = (PART, rows_dev + 16 - PART)

    def part_of(g, back_u, back_v, start=0, size=None):
        x_at, y_at = cross(g, mod(uv[g][0] + back_u), mod(uv[g][1] + back_v))
        return slots.at[x_at * RING + y_at, pl.ds(g * PART + start, sizes[g] if size is None else size)]

    def plane_device(g, ahead_u, ahead_v):
        return device(*cross(g, mod(uv[g][0] + ahead_u), mod(uv[g][1] + ahead_v)), z, k)

    def remote(src, dst, send, recv, to):
        return pltpu.make_async_remote_copy(
            src_ref=src, dst_ref=dst, send_sem=send, recv_sem=recv, device_id=to, device_id_type=MESH
        )

    def arrival(dst, send, recv):
        remote(dst, dst, send, recv, mate).wait_recv()

    load_a = pltpu.make_async_copy(fit_a, a_own, load_sem.at[0])
    load_b = pltpu.make_async_copy(fit_b.at[pl.ds(k * B_CORE, B_CORE)], b_own, load_sem.at[1])
    load_t = pltpu.make_async_copy(tiles, slots.at[me, pl.ds(0, rows_dev)], load_sem.at[2])
    load_o = pltpu.make_async_copy(owner, owners, load_sem.at[3])
    load_u = pltpu.make_async_copy(sub_block, subs, load_sem.at[4])
    for load in (load_o, load_u, load_t, load_a, load_b):
        load.start()

    load_o.wait()
    load_u.wait()
    spot = (owners[...] * BLOCKS_OWNER + subs[...]) * 8 + lax.div(
        lax.broadcasted_iota(jnp.int32, owners.shape, 1), TILES_PAIR
    )
    slots[me, rows_dev : rows_dev + 16, :] = jnp.concatenate([spot, spot], axis=0).astype(F32).astype(BF16)
    row_ids[...] = lax.broadcasted_iota(jnp.int32, row_ids.shape, 0).astype(F32).astype(BF16)

    barrier = pltpu.get_barrier_semaphore()

    def greet(i, carry):
        to = device(mod(x + lax.div(i, RING)), mod(y + lax.rem(i, RING)), z, k)
        pl.semaphore_signal(barrier, inc=1, device_id=to, device_id_type=MESH)
        return carry

    for to in (mate, along(0), along(1)):
        pl.semaphore_signal(barrier, inc=1, device_id=to, device_id_type=MESH)
    lax.fori_loop(1, PLANE, greet, 0)
    pl.semaphore_wait(barrier, PLANE + 2)

    def swap_a(i):
        rows = pl.ds(pl.multiple_of(mod(z + (2, 1, 3, 0)[i]) * ROWS, ROWS), ROWS)
        return remote(fit_a.at[rows], a_mate.at[rows], mate_s.at[i], mate_r.at[i], mate)

    def swap_b(i):
        first, count = ((0, 2), (2, 2), (4, 4))[i]
        here, there = pl.ds((1 - k) * B_CORE + first, count), pl.ds(first, count)
        return remote(fit_b.at[here], b_mate.at[there], mate_s.at[4 + i], mate_r.at[4 + i], mate)

    for swap in (swap_a(0), swap_b(0), swap_b(1), swap_a(1), swap_a(2), swap_b(2), swap_a(3)):
        swap.start()

    def ring1(g, d):
        ref = part_of(g, 0, 0)
        return remote(ref, ref, ring1_s.at[g, d], ring1_r.at[g, d], plane_device(g, 1 + 2 * d, 0))

    def half_ref(g, d, back):
        first = sizes[g] // 32 * 16
        return part_of(g, back, 0, d * first, sizes[g] - first if d else first)

    def half1(g, d):
        ref = half_ref(g, d, 3 - 2 * d)
        return remote(ref, ref, half1_s.at[g, d], half1_r.at[g, d], plane_device(g, 1 + 2 * d, 0))

    def ring2(g, d, i):
        ref = part_of(g, i, 0)
        return remote(ref, ref, ring2_s.at[g, d, i], ring2_r.at[g, d, i], plane_device(g, 0, 1 + 2 * d))

    def pass2(g, i):
        d = i // 2
        ref = part_of(g, i, 3 - 2 * d)
        return remote(ref, ref, pass2_s.at[g, i], pass2_r.at[g, i], plane_device(g, 0, 1 + 2 * d))

    def both_ways(i):
        for g in range(2):
            for d in (0, 1):
                ring2(g, d, i).start()

    def pass_on(d, i):
        for g in range(2):
            arrival(part_of(g, i, 3 - 2 * d), ring2_s.at[g, d, i], ring2_r.at[g, d, i])
            if i // 2 == d:
                pass2(g, i).start()

    load_t.wait()
    for g in range(2):
        for d in (0, 1):
            ring1(g, d).start()
    both_ways(0)
    load_a.wait()
    load_b.wait()

    def partial(part, h, t):
        rows = pl.ds(pl.multiple_of(part * ROWS, ROWS), ROWS)
        b = t * 4 + h * 2
        own = product(a_own[rows, :], jnp.concatenate([b_own[b], b_own[b + 1]], axis=1), 0)
        return own + product(a_mate[rows, :], jnp.concatenate([b_mate[b], b_mate[b + 1]], axis=1), 0)

    def far_copy(s, d):
        return remote(far_out.at[s, d], far_in.at[s, d], far_s.at[s, d], far_r.at[s, d], along(d))

    def side_copy(s, d):
        return remote(side_out.at[s, d], side_in.at[s, d], side_s.at[s, d], side_r.at[s, d], along(d))

    def comb_copy(s, d):
        return remote(comb_out.at[s, d], comb_in.at[s, d], comb_s.at[s, d], comb_r.at[s, d], along(d))

    def x_copy(s, i):
        rows = pl.ds(i * X_ROWS, X_ROWS)
        return remote(x_out.at[s, rows], x_in.at[s, rows], x_s.at[s, i], x_r.at[s, i], partner)

    def keep(ref, t, d, value):
        ref[2 * t, d] = value[:, :ND].astype(ref.dtype)
        ref[2 * t + 1, d] = value[:, ND:].astype(ref.dtype)

    def far_piece(t, d):
        keep(far_out, t, d, partial(far, d, t))

    def side_piece(t, d):
        keep(side_out, t, d, partial(mod(z + 1 + 2 * d), 1 - d, t))

    def comb_piece(t, d):
        keep(keep_comb, t, d, partial(mod(z + 1 + 2 * d), d, t))

    def own_piece(t, d):
        keep(keep_own, t, d, partial(z, d, t))

    def each_way(t, piece):
        def one(d, carry):
            piece(t, d)
            return carry

        lax.fori_loop(0, 2, one, 0)

    def both(s, copy):
        copy(s, 0).start()
        copy(s, 1).start()

    def send_comb(s):
        for d in (0, 1):
            far_copy(s, d).wait_recv()
            comb_out[s, d] = (keep_comb[s, d] + far_in[s, d].astype(F32)).astype(BF16)
            comb_copy(s, d).start()

    def build(slot):
        names[...] = slots[slot, pl.ds(rows_dev, 16), :].astype(F32)
        none = jnp.zeros((128, ND), BF16)

        def chosen(row):
            line = jnp.broadcast_to(names[row : row + 1, :], (16, 128)).astype(BF16)
            return jnp.where(row_ids[...] == jnp.concatenate([line] * 16, axis=0), 1.0, 0.0).astype(BF16)

        for j in range(rows_dev // STEP):
            choice = jnp.concatenate([chosen(2 * j), chosen(2 * j + 1)], axis=1)
            first = slots[slot, j * STEP : j * STEP + 128, :]
            second = slots[slot, j * STEP + 128 : (j + 1) * STEP, :]
            values = jnp.concatenate(
                [jnp.concatenate([first, none], axis=1), jnp.concatenate([none, second], axis=1)], axis=0
            )
            sums = product(choice, values, 0)
            rows = pl.ds(pl.multiple_of(slot * pairs_dev + j * 16, 16), 16)
            for c in range(NC):
                part = sums[c * 8 : (c + 1) * 8]
                part = jnp.concatenate([part[:, :ND], part[:, ND:]], axis=0)
                summed[c // 4, rows, (c % 4) * ND : (c % 4 + 1) * ND] = part.astype(BF16)

    def build_near(dx, first, last):
        def one(i, carry):
            build(mod(x + dx) * RING + mod(y + i + i // 2))
            return carry

        lax.fori_loop(first, last, one, 0)

    def build_far(first, last):
        def one(i, carry):
            build(mod(x + 2) * RING + mod(y + i))
            return carry

        lax.fori_loop(first, last, one, 0)

    def send_x(s):
        comb_copy(s, 0).wait_recv()
        comb_copy(s, 1).wait_recv()
        side_copy(s, 0).wait_recv()
        side_copy(s, 1).wait_recv()
        h = 1 - x_lo
        x_out[s] = (keep_own[s, h] + comb_in[s, h].astype(F32) + side_in[s, 1 - h].astype(F32)).astype(BF16)
        for i in range(X_PARTS):
            x_copy(s, i).start()

    def ag_copy(s, d):
        ref = ints.at[s, z, k]
        return remote(ref, ref, ag_s.at[s, d], ag_r.at[s, d], along(d))

    def fw_ref(s, part, core, d):
        return ints.at[s, part, core, :, pl.ds(d * STEP, STEP)]

    def fw_copy(s, d):
        ref = fw_ref(s, mod(z + 3 - 2 * d), k, d)
        return remote(ref, ref, fw_s.at[s, d], fw_r.at[s, d], along(d))

    def cx_ref(s, i, core):
        if i < 3:
            return ints.at[s, (z, down, up)[i], core]
        return fw_ref(s, far, core, i - 3)

    def cx_copy(s, i):
        ref = cx_ref(s, i, k)
        return remote(ref, ref, cx_s.at[s, i], cx_r.at[s, i], mate)

    def finish(s):
        for i in range(X_PARTS):
            x_copy(s, i).wait_recv()
        h = x_lo
        blocks = []
        for two in range(C_PART // 2):
            rows = pl.ds(two * 2 * NA, 2 * NA)
            value = (
                keep_own[s, h, rows, :]
                + comb_in[s, h, rows, :].astype(F32)
                + side_in[s, 1 - h, rows, :].astype(F32)
                + x_in[s, rows, :].astype(F32)
            )
            blocks += [value[:NA], value[NA:]]
        lines = [jnp.concatenate(blocks[i * 4 : i * 4 + 4], axis=1) for i in range(2)]
        ints[s, z, k] = jnp.concatenate(lines, axis=0).astype(BF16)
        ag_copy(s, 0).start()
        ag_copy(s, 1).start()
        cx_copy(s, 0).start()

    def forward(s):
        for d in (0, 1):
            from_z = mod(z + 3 - 2 * d)
            arrival(ints.at[s, from_z, k], ag_s.at[s, d], ag_r.at[s, d])
            fw_copy(s, d).start()
            cx_copy(s, 1 + d).start()

    def last_forward(s):
        for d in (0, 1):
            arrival(fw_ref(s, far, k, d), fw_s.at[s, d], fw_r.at[s, d])
            cx_copy(s, 3 + d).start()

    def multiply(t, part, first):
        left = [[], []]
        for s in (2 * t, 2 * t + 1):
            for core in range(CORES):
                value = ints[s, part, core].astype(F32)
                left[0].append(value[:NA])
                left[1].append(value[NA:])
        left = [jnp.concatenate(value, axis=0).astype(BF16) for value in left]

        def one(n, carry):
            rows = pl.ds(pl.multiple_of(n * 512, 512), 512)
            value = product(summed[part * 2, rows, :], left[0], 1) + product(summed[part * 2 + 1, rows, :], left[1], 1)
            total[t, rows, : 4 * NA] = value if first else total[t, rows, : 4 * NA] + value
            return carry

        lax.fori_loop(0, total.shape[1] // 512, one, 0)

    def gathered(t, i):
        for s in (2 * t, 2 * t + 1):
            arrival(cx_ref(s, i, 1 - k), cx_s.at[s, i], cx_r.at[s, i])
            if i == 3:
                arrival(cx_ref(s, 4, 1 - k), cx_s.at[s, 4], cx_r.at[s, 4])
        multiply(t, (z, down, up, far)[i], i == 0)

    def out_copy(t, i):
        x_at, y_at = mod(x + i // RING), mod(y + i % RING)
        return remote(
            parcels.at[t, x_at * RING + y_at], got.at[t, me], out_s.at[t, i], out_r.at[t, i], device(x_at, y_at, z, k)
        )

    def send_out(t):
        low = lax.broadcasted_iota(jnp.int32, (OUT_ROWS, 128), 1) < 64
        for n in range(PLANE // 2):
            rows = slice(n * 128, (n + 1) * 128)
            value = jnp.concatenate([total[t, rows, :128].T, total[t, rows, 128:].T[: 4 * NA - 128]], axis=0)
            top = jnp.concatenate([value[i * NA : i * NA + A_HALF] for i in range(4)], axis=0)
            bottom = jnp.concatenate([value[i * NA + A_HALF : (i + 1) * NA] for i in range(4)], axis=0)
            parcels[t, 2 * n] = jnp.where(low, top, pltpu.roll(bottom, 64, 1)).astype(BF16)
            parcels[t, 2 * n + 1] = jnp.where(low, pltpu.roll(top, 64, 1), bottom).astype(BF16)

        for i in FARTHEST_FIRST:
            out_copy(t, i).start()

    def unpack(t, x_at, y_at, value):
        base = (lax.div(x_at, 2) * RING + y_at) * 16 + t * 4 + lax.rem(x_at, 2) * 2
        for at in range(4):
            rows = pl.ds(pl.multiple_of((base + at % 2 * 8 + at // 2) * B_STRIDE, 8), A_HALF)
            final[rows, :] = value[at * A_HALF : (at + 1) * A_HALF]

    def receive(t):
        unpack(t, x, y, parcels[t, me].astype(F32))

        for i in FARTHEST_FIRST:
            x_at, y_at = mod(x + RING - i // RING), mod(y + RING - i % RING)
            slot = x_at * RING + y_at
            arrival(got.at[t, slot], out_s.at[t, i], out_r.at[t, i])
            unpack(t, x_at, y_at, got[t, slot].astype(F32))

    swap_a(0).wait_recv()
    for d in (0, 1):
        swap_b(d).wait_recv()
        far_piece(0, d)
        far_copy(0, d).start()
        far_copy(1, d).start()
    swap_a(1).wait_recv()
    swap_a(2).wait_recv()
    each_way(0, side_piece)
    both(0, side_copy)
    each_way(0, comb_piece)
    for g in range(2):
        for d in (0, 1):
            arrival(part_of(g, 3 - 2 * d, 0), ring1_s.at[g, d], ring1_r.at[g, d])
            half1(g, d).start()
    both_ways(3)
    both_ways(1)
    swap_b(2).wait_recv()
    swap_a(3).wait_recv()
    each_way(1, far_piece)
    send_comb(0)
    both(1, side_copy)
    send_comb(1)
    both(2, far_copy)
    both(3, far_copy)
    for g in range(2):
        for d in (0, 1):
            arrival(half_ref(g, d, 2), half1_s.at[g, d], half1_r.at[g, d])
    both_ways(2)
    each_way(1, side_piece)
    both(2, side_copy)
    each_way(1, comb_piece)
    each_way(0, own_piece)
    each_way(1, own_piece)
    send_x(0)
    pass_on(0, 0)
    pass_on(1, 3)
    build_near(0, 0, 1)
    send_x(1)
    pass_on(0, 1)
    send_comb(2)
    both(3, side_copy)
    pass_on(1, 2)
    for d, i in ((0, 3), (0, 2), (1, 0), (1, 1)):
        pass_on(d, i)
    send_comb(3)
    build_near(0, 1, 3)
    finish(0)
    build_near(1, 0, 3)
    finish(1)
    send_x(2)
    build_near(3, 0, 3)
    send_x(3)
    finish(2)
    for g in range(2):
        for i in range(RING):
            arrival(part_of(g, i, 2), pass2_s.at[g, i], pass2_r.at[g, i])
    build_far(0, RING)
    forward(0)
    for dx in (0, 1, 3):
        build(mod(x + dx) * RING + mod(y + 2))
    forward(1)
    finish(3)
    gathered(0, 0)
    gathered(0, 1)
    forward(2)
    gathered(0, 2)
    last_forward(0)
    last_forward(1)
    gathered(1, 0)
    forward(3)
    gathered(0, 3)
    send_out(0)
    last_forward(2)
    gathered(1, 1)
    last_forward(3)
    gathered(1, 2)
    gathered(1, 3)
    send_out(1)
    for t in range(GROUPS):
        receive(t)
    for i in range(A_HALF):
        value = final[pl.ds(i, NB, stride=B_STRIDE), :]
        turned = value.T.astype(BF16)
        out[:, i * NB : (i + 1) * NB] = turned[:pairs_dev]
        out[:, (i + A_HALF) * NB : (i + A_HALF + 1) * NB] = turned[pairs_dev:]

    for i in range(RING):
        swap_a(i).wait_send()
    for i in range(3):
        swap_b(i).wait_send()
    for g in range(2):
        for d in (0, 1):
            ring1(g, d).wait_send()
            half1(g, d).wait_send()
            for i in range(RING):
                ring2(g, d, i).wait_send()
        for i in range(RING):
            pass2(g, i).wait_send()
    for s in range(SLICES):
        for i in range(X_PARTS):
            x_copy(s, i).wait_send()
        for d in (0, 1):
            far_copy(s, d).wait_send()
            side_copy(s, d).wait_send()
            comb_copy(s, d).wait_send()
            ag_copy(s, d).wait_send()
            fw_copy(s, d).wait_send()
        for i in range(5):
            cx_copy(s, i).wait_send()

    for t in range(GROUPS):
        for i in FARTHEST_FIRST:
            out_copy(t, i).wait_send()


def on_device(tiles, owner, sub_block, fit_ac, fit_bd):
    rows_dev = tiles.shape[0]
    depth = fit_ac.shape[2]
    owner = owner.reshape(rows_dev // 128, 128)
    sub_block = sub_block.reshape(rows_dev // 128, 128)
    fit_a = fit_ac.reshape(NC * NA, depth)
    fit_b = jnp.swapaxes(fit_bd, 1, 2)
    pairs = rows_dev // TILES_PAIR * PLANE
    dma = pltpu.SemaphoreType.DMA
    return pl.pallas_call(
        kernel,
        out_shape=pltpu.VMEM((rows_dev // TILES_PAIR, NA * NB), BF16),
        in_specs=[pl.BlockSpec(memory_space=pl.ANY)] * 5,
        out_specs=pl.BlockSpec(memory_space=pltpu.VMEM),
        scratch_shapes=[
            pltpu.VMEM((NC * NA, depth), BF16),
            pltpu.VMEM((NC * NA, depth), BF16),
            pltpu.VMEM((B_CORE, depth, ND), BF16),
            pltpu.VMEM((B_CORE, depth, ND), BF16),
            pltpu.VMEM((PLANE, rows_dev + 16, ND), BF16),
            *[pltpu.VMEM((SLICES, 2, ROWS, ND), BF16)] * 6,
            *[pltpu.VMEM((SLICES, 2, ROWS, ND), F32)] * 2,
            *[pltpu.VMEM((SLICES, ROWS, ND), BF16)] * 2,
            pltpu.VMEM((SLICES, RING, CORES, 2 * NA, K_HALF), BF16),
            pltpu.VMEM((2 * RING, pairs, K_HALF), BF16),
            pltpu.VMEM((GROUPS, pairs, STEP), F32),
            *[pltpu.VMEM((GROUPS, PLANE, OUT_ROWS, 128), BF16)] * 2,
            *[pltpu.VMEM((rows_dev // 128, 128), jnp.int32)] * 2,
            pltpu.VMEM((STEP, 128), BF16),
            pltpu.VMEM((16, 128), F32),
            pltpu.VMEM((NB * B_STRIDE, 128), F32),
            dma((5,)),
            dma((7,)), dma((7,)),
            *[dma((2, 2))] * 4,
            *[dma((2, 2, RING))] * 2,
            *[dma((2, RING))] * 2,
            *[dma((SLICES, 2))] * 6,
            *[dma((SLICES, X_PARTS))] * 2,
            *[dma((SLICES, 2))] * 4,
            *[dma((SLICES, 5))] * 2,
            *[dma((GROUPS, PLANE))] * 2,
        ],
        compiler_params=pltpu.CompilerParams(
            collective_id=0, has_side_effects=True, vmem_limit_bytes=56 * 1024 * 1024
        ),
        cost_estimate=pl.CostEstimate(flops=7 * 10**9, bytes_accessed=4 * 10**6, transcendentals=0),
        name="ladder",
    )(tiles, owner, sub_block, fit_a, fit_b)


def solution(mesh):
    placed = (
        P(("blk", "occ"), None),
        P(("blk", "occ"), None),
        P(("blk", "occ")),
        P(None, None, "occ"),
        P("blk", None, "occ"),
    )
    return jax.shard_map(
        on_device, mesh=mesh, in_specs=placed, out_specs=P(("blk", "occ"), None), check_vma=False
    )
```

```python
import jax
import jax.numpy as jnp
from jax import lax
from jax.experimental import pallas as pl
from jax.experimental.pallas import tpu as pltpu
from jax.sharding import PartitionSpec as P

MESH = pl.DeviceIdType.MESH
RING = 4
CORES = 2
SLICES = 4
GROUPS = 2
TILES_PAIR = 16
NA, NB, NC, ND = 40, 128, 32, 128
BLOCKS_OWNER = 2
PLANE = RING * RING
A_HALF = NA // 2
PART = 640
C_PART = NC // RING
ROWS = C_PART * NA
B_CORE = 8
X_PARTS = 1
X_ROWS = ROWS // X_PARTS
K_HALF = C_PART * ND // 2
OUT_ROWS = 2 * CORES * A_HALF
B_STRIDE = 24
STEP = 256
FARTHEST_FIRST = ((10, 9, 6, 11, 8, 5, 7, 4), (14, 2, 15, 13, 1, 12, 3))

F32, BF16 = jnp.float32, jnp.bfloat16


def product(left, right, right_axis):
    return lax.dot_general(left, right, (((1,), (right_axis,)), ((), ())), preferred_element_type=F32)


def kernel(
    tiles, owner, sub_block, fit_a, fit_b, out,
    a_own, a_mate, b_own, b_mate, slots, far_out, side_out, comb_out, far_in, side_in, comb_in,
    keep_comb, keep_own, x_out, x_in, ints, summed, total, parcels, got, owners, subs, row_ids, names, final,
    load_sem, mate_s, mate_r, ring1_s, ring1_r, half1_s, half1_r, ring2_s, ring2_r, pass2_s, pass2_r,
    far_s, far_r, side_s, side_r, comb_s, comb_r, x_s, x_r, ag_s, ag_r, fw_s, fw_r, cx_s, cx_r, out_s, out_r,
):
    blk, occ = lax.axis_index("blk"), lax.axis_index("occ")
    x_hi, y = lax.div(blk, RING), lax.rem(blk, RING)
    z, x_lo, k = lax.div(occ, 4), lax.rem(lax.div(occ, 2), 2), lax.rem(occ, 2)
    x = x_hi * 2 + x_lo
    rows_dev = tiles.shape[0]
    pairs_dev = rows_dev // TILES_PAIR

    def mod(value):
        return lax.rem(value, RING)

    def device(x_at, y_at, z_at, k_at):
        return (lax.div(x_at, 2) * RING + y_at, z_at * 4 + lax.rem(x_at, 2) * 2 + k_at)

    up, down, far = mod(z + 1), mod(z + 3), mod(z + 2)
    mate = device(x, y, z, 1 - k)
    partner = device(x_hi * 2 + 1 - x_lo, y, z, k)

    def along(d):
        return device(x, y, mod(z + 1 + 2 * d), k)

    me = x * RING + y
    def cross(g, u_at, v_at):
        return (u_at, v_at) if g == 0 else (v_at, u_at)

    uv = (cross(0, x, y), cross(1, x, y))

    sizes = (PART, rows_dev + 16 - PART)

    def part_of(g, back_u, back_v, start=0, size=None):
        x_at, y_at = cross(g, mod(uv[g][0] + back_u), mod(uv[g][1] + back_v))
        return slots.at[x_at * RING + y_at, pl.ds(g * PART + start, sizes[g] if size is None else size)]

    def plane_device(g, ahead_u, ahead_v):
        return device(*cross(g, mod(uv[g][0] + ahead_u), mod(uv[g][1] + ahead_v)), z, k)

    def remote(src, dst, send, recv, to):
        return pltpu.make_async_remote_copy(
            src_ref=src, dst_ref=dst, send_sem=send, recv_sem=recv, device_id=to, device_id_type=MESH
        )

    def arrival(dst, send, recv):
        remote(dst, dst, send, recv, mate).wait_recv()

    load_a = pltpu.make_async_copy(fit_a, a_own, load_sem.at[0])
    load_b = pltpu.make_async_copy(fit_b.at[pl.ds(k * B_CORE, B_CORE)], b_own, load_sem.at[1])
    load_t = pltpu.make_async_copy(tiles, slots.at[me, pl.ds(0, rows_dev)], load_sem.at[2])
    load_o = pltpu.make_async_copy(owner, owners, load_sem.at[3])
    load_u = pltpu.make_async_copy(sub_block, subs, load_sem.at[4])
    for load in (load_o, load_u, load_t, load_a, load_b):
        load.start()

    barrier = pltpu.get_barrier_semaphore()

    def greet(i, carry):
        to = device(mod(x + lax.div(i, RING)), mod(y + lax.rem(i, RING)), z, k)
        pl.semaphore_signal(barrier, inc=1, device_id=to, device_id_type=MESH)
        return carry

    across = device(x, y, far, k)
    for to in (mate, along(0), along(1), across):
        pl.semaphore_signal(barrier, inc=1, device_id=to, device_id_type=MESH)
    lax.fori_loop(1, PLANE, greet, 0)
    load_o.wait()
    load_u.wait()
    spot = (owners[...] * BLOCKS_OWNER + subs[...]) * 8 + lax.div(
        lax.broadcasted_iota(jnp.int32, owners.shape, 1), TILES_PAIR
    )
    slots[me, rows_dev : rows_dev + 16, :] = jnp.concatenate([spot, spot], axis=0).astype(F32).astype(BF16)
    row_ids[...] = lax.broadcasted_iota(jnp.int32, row_ids.shape, 0).astype(F32).astype(BF16)

    pl.semaphore_wait(barrier, PLANE + 3)

    def swap_a(i):
        rows = pl.ds(pl.multiple_of(mod(z + (2, 1, 3, 0)[i]) * ROWS, ROWS), ROWS)
        return remote(fit_a.at[rows], a_mate.at[rows], mate_s.at[i], mate_r.at[i], mate)

    def swap_b(i):
        first, count = ((0, 2), (2, 2), (4, 4))[i]
        here, there = pl.ds((1 - k) * B_CORE + first, count), pl.ds(first, count)
        return remote(fit_b.at[here], b_mate.at[there], mate_s.at[4 + i], mate_r.at[4 + i], mate)

    for swap in (swap_a(0), swap_b(0), swap_b(1), swap_a(1), swap_a(2), swap_b(2), swap_a(3)):
        swap.start()

    def ring1(g, d):
        ref = part_of(g, 0, 0)
        return remote(ref, ref, ring1_s.at[g, d], ring1_r.at[g, d], plane_device(g, 1 + 2 * d, 0))

    def half_ref(g, d, back):
        first = sizes[g] // 32 * 16
        return part_of(g, back, 0, d * first, sizes[g] - first if d else first)

    def half1(g, d):
        ref = half_ref(g, d, 3 - 2 * d)
        return remote(ref, ref, half1_s.at[g, d], half1_r.at[g, d], plane_device(g, 1 + 2 * d, 0))

    def ring2(g, d, i):
        ref = part_of(g, i, 0)
        return remote(ref, ref, ring2_s.at[g, d, i], ring2_r.at[g, d, i], plane_device(g, 0, 1 + 2 * d))

    def pass2(g, i):
        d = i // 2
        ref = part_of(g, i, 3 - 2 * d)
        return remote(ref, ref, pass2_s.at[g, i], pass2_r.at[g, i], plane_device(g, 0, 1 + 2 * d))

    def both_ways(i):
        for g in range(2):
            for d in (0, 1):
                ring2(g, d, i).start()

    def pass_on(d, i):
        for g in range(2):
            arrival(part_of(g, i, 3 - 2 * d), ring2_s.at[g, d, i], ring2_r.at[g, d, i])
            if i // 2 == d:
                pass2(g, i).start()

    load_t.wait()
    for g in range(2):
        for d in (0, 1):
            ring1(g, d).start()
    both_ways(0)
    load_a.wait()
    load_b.wait()

    def partial(part, h, t):
        rows = pl.ds(pl.multiple_of(part * ROWS, ROWS), ROWS)
        b = t * 4 + h * 2
        own = product(a_own[rows, :], jnp.concatenate([b_own[b], b_own[b + 1]], axis=1), 0)
        return own + product(a_mate[rows, :], jnp.concatenate([b_mate[b], b_mate[b + 1]], axis=1), 0)

    def far_copy(s, d):
        return remote(far_out.at[s, d], far_in.at[s, d], far_s.at[s, d], far_r.at[s, d], along(d))

    def side_copy(s, d):
        return remote(side_out.at[s, d], side_in.at[s, d], side_s.at[s, d], side_r.at[s, d], along(d))

    def comb_copy(s, d):
        return remote(comb_out.at[s, d], comb_in.at[s, d], comb_s.at[s, d], comb_r.at[s, d], along(d))

    def x_copy(s, i):
        rows = pl.ds(i * X_ROWS, X_ROWS)
        return remote(x_out.at[s, rows], x_in.at[s, rows], x_s.at[s, i], x_r.at[s, i], partner)

    def keep(ref, t, d, value):
        ref[2 * t, d] = value[:, :ND].astype(ref.dtype)
        ref[2 * t + 1, d] = value[:, ND:].astype(ref.dtype)

    def far_piece(t, d):
        keep(far_out, t, d, partial(far, d, t))

    def side_piece(t, d):
        keep(side_out, t, d, partial(mod(z + 1 + 2 * d), 1 - d, t))

    def comb_piece(t, d):
        keep(keep_comb, t, d, partial(mod(z + 1 + 2 * d), d, t))

    def own_piece(t, d):
        keep(keep_own, t, d, partial(z, d, t))

    def each_way(t, piece):
        def one(d, carry):
            piece(t, d)
            return carry

        lax.fori_loop(0, 2, one, 0)

    def both(s, copy):
        copy(s, 0).start()
        copy(s, 1).start()

    def send_comb(s):
        for d in (0, 1):
            far_copy(s, d).wait_recv()
            comb_out[s, d] = (keep_comb[s, d] + far_in[s, d].astype(F32)).astype(BF16)
            comb_copy(s, d).start()

    def build(slot):
        names[...] = slots[slot, pl.ds(rows_dev, 16), :].astype(F32)
        none = jnp.zeros((128, ND), BF16)

        def chosen(row):
            line = jnp.broadcast_to(names[row : row + 1, :], (16, 128)).astype(BF16)
            return jnp.where(row_ids[...] == jnp.concatenate([line] * 16, axis=0), 1.0, 0.0).astype(BF16)

        for j in range(rows_dev // STEP):
            choice = jnp.concatenate([chosen(2 * j), chosen(2 * j + 1)], axis=1)
            first = slots[slot, j * STEP : j * STEP + 128, :]
            second = slots[slot, j * STEP + 128 : (j + 1) * STEP, :]
            values = jnp.concatenate(
                [jnp.concatenate([first, none], axis=1), jnp.concatenate([none, second], axis=1)], axis=0
            )
            sums = product(choice, values, 0)
            rows = pl.ds(pl.multiple_of(slot * pairs_dev + j * 16, 16), 16)
            for c in range(NC):
                part = sums[c * 8 : (c + 1) * 8]
                part = jnp.concatenate([part[:, :ND], part[:, ND:]], axis=0)
                summed[c // 4, rows, (c % 4) * ND : (c % 4 + 1) * ND] = part.astype(BF16)

    def build_near(dx, first, last):
        def one(i, carry):
            build(mod(x + dx) * RING + mod(y + i + i // 2))
            return carry

        lax.fori_loop(first, last, one, 0)

    def build_far(first, last):
        def one(i, carry):
            build(mod(x + 2) * RING + mod(y + i))
            return carry

        lax.fori_loop(first, last, one, 0)

    def send_x(s):
        comb_copy(s, 0).wait_recv()
        comb_copy(s, 1).wait_recv()
        side_copy(s, 0).wait_recv()
        side_copy(s, 1).wait_recv()
        h = 1 - x_lo
        x_out[s] = (keep_own[s, h] + comb_in[s, h].astype(F32) + side_in[s, 1 - h].astype(F32)).astype(BF16)
        for i in range(X_PARTS):
            x_copy(s, i).start()

    def ag_copy(s, d):
        ref = ints.at[s, z, k]
        return remote(ref, ref, ag_s.at[s, d], ag_r.at[s, d], along(d))

    def fw_ref(s, part, core, d):
        return ints.at[s, part, core, :, pl.ds(d * STEP, STEP)]

    def fw_copy(s, d):
        ref = fw_ref(s, mod(z + 3 - 2 * d), k, d)
        return remote(ref, ref, fw_s.at[s, d], fw_r.at[s, d], along(d))

    def across_copy(s):
        ref = ints.at[s, z, k]
        return remote(ref, ref, fw_s.at[s, 0], fw_r.at[s, 0], across)

    def cx_ref(s, i, core):
        if i < 3:
            return ints.at[s, (z, down, up)[i], core]
        return fw_ref(s, far, core, i - 3)

    def cx_copy(s, i):
        ref = cx_ref(s, i, k)
        return remote(ref, ref, cx_s.at[s, i], cx_r.at[s, i], mate)

    def finish(s):
        for i in range(X_PARTS):
            x_copy(s, i).wait_recv()
        h = x_lo
        blocks = []
        for two in range(C_PART // 2):
            rows = pl.ds(two * 2 * NA, 2 * NA)
            value = (
                keep_own[s, h, rows, :]
                + comb_in[s, h, rows, :].astype(F32)
                + side_in[s, 1 - h, rows, :].astype(F32)
                + x_in[s, rows, :].astype(F32)
            )
            blocks += [value[:NA], value[NA:]]
        lines = [jnp.concatenate(blocks[i * 4 : i * 4 + 4], axis=1) for i in range(2)]
        ints[s, z, k] = jnp.concatenate(lines, axis=0).astype(BF16)
        ag_copy(s, 0).start()
        ag_copy(s, 1).start()
        cx_copy(s, 0).start()

    def forward(s):
        for d in (0, 1):
            from_z = mod(z + 3 - 2 * d)
            arrival(ints.at[s, from_z, k], ag_s.at[s, d], ag_r.at[s, d])
            if s < SLICES - 1:
                fw_copy(s, d).start()
            cx_copy(s, 1 + d).start()

    def last_forward(s):
        for d in (0, 1):
            if s < SLICES - 1:
                arrival(fw_ref(s, far, k, d), fw_s.at[s, d], fw_r.at[s, d])
            elif d == 0:
                arrival(ints.at[s, far, k], fw_s.at[s, 0], fw_r.at[s, 0])
            cx_copy(s, 3 + d).start()

    def multiply(t, part, first):
        left = [[], []]
        for s in (2 * t, 2 * t + 1):
            for core in range(CORES):
                value = ints[s, part, core].astype(F32)
                left[0].append(value[:NA])
                left[1].append(value[NA:])
        left = [jnp.concatenate(value, axis=0).astype(BF16) for value in left]

        def one(n, carry):
            rows = pl.ds(pl.multiple_of(n * 512, 512), 512)
            value = product(summed[part * 2, rows, :], left[0], 1) + product(summed[part * 2 + 1, rows, :], left[1], 1)
            total[t, rows, : 4 * NA] = value if first else total[t, rows, : 4 * NA] + value
            return carry

        lax.fori_loop(0, total.shape[1] // 512, one, 0)

    def await_gathered(t, i):
        for s in (2 * t, 2 * t + 1):
            arrival(cx_ref(s, i, 1 - k), cx_s.at[s, i], cx_r.at[s, i])
            if i == 3:
                arrival(cx_ref(s, 4, 1 - k), cx_s.at[s, 4], cx_r.at[s, 4])

    def gathered(t, i):
        await_gathered(t, i)
        multiply(t, (z, down, up, far)[i], i == 0)

    def finish_out(t):
        gathered(t, 3)
        send_out(t)

    def out_copy(t, i):
        x_at, y_at = mod(x + i // RING), mod(y + i % RING)
        return remote(
            parcels.at[t, x_at * RING + y_at], got.at[t, me], out_s.at[t, i], out_r.at[t, i], device(x_at, y_at, z, k)
        )

    def send_out(t):
        low = lax.broadcasted_iota(jnp.int32, (OUT_ROWS, 128), 1) < 64
        for n in range(PLANE // 2):
            rows = slice(n * 128, (n + 1) * 128)
            value = jnp.concatenate([total[t, rows, :128].T, total[t, rows, 128:].T[: 4 * NA - 128]], axis=0)
            top = jnp.concatenate([value[i * NA : i * NA + A_HALF] for i in range(4)], axis=0)
            bottom = jnp.concatenate([value[i * NA + A_HALF : (i + 1) * NA] for i in range(4)], axis=0)
            parcels[t, 2 * n] = jnp.where(low, top, pltpu.roll(bottom, 64, 1)).astype(BF16)
            parcels[t, 2 * n + 1] = jnp.where(low, pltpu.roll(top, 64, 1), bottom).astype(BF16)
        for i in FARTHEST_FIRST[0] + FARTHEST_FIRST[1]:
            out_copy(t, i).start()

    def unpack(t, x_at, y_at, value):
        base = (lax.div(x_at, 2) * RING + y_at) * 16 + t * 4 + lax.rem(x_at, 2) * 2
        for at in range(4):
            rows = pl.ds(pl.multiple_of((base + at % 2 * 8 + at // 2) * B_STRIDE, 8), A_HALF)
            final[rows, :] = value[at * A_HALF : (at + 1) * A_HALF]

    def receive(t):
        unpack(t, x, y, parcels[t, me].astype(F32))

        for i in FARTHEST_FIRST[0] + FARTHEST_FIRST[1]:
            x_at, y_at = mod(x + RING - i // RING), mod(y + RING - i % RING)
            slot = x_at * RING + y_at
            arrival(got.at[t, slot], out_s.at[t, i], out_r.at[t, i])
            unpack(t, x_at, y_at, got[t, slot].astype(F32))

    swap_a(0).wait_recv()
    for d in (0, 1):
        swap_b(d).wait_recv()
        far_piece(0, d)
        far_copy(0, d).start()
        far_copy(1, d).start()
    swap_a(1).wait_recv()
    swap_a(2).wait_recv()
    each_way(0, side_piece)
    both(0, side_copy)
    each_way(0, comb_piece)
    for g in range(2):
        for d in (0, 1):
            arrival(part_of(g, 3 - 2 * d, 0), ring1_s.at[g, d], ring1_r.at[g, d])
            half1(g, d).start()
    both_ways(3)
    both_ways(1)
    swap_b(2).wait_recv()
    swap_a(3).wait_recv()
    each_way(1, far_piece)
    send_comb(0)
    both(1, side_copy)
    send_comb(1)
    both(2, far_copy)
    both(3, far_copy)
    for g in range(2):
        for d in (0, 1):
            arrival(half_ref(g, d, 2), half1_s.at[g, d], half1_r.at[g, d])
    both_ways(2)
    each_way(1, side_piece)
    both(2, side_copy)
    each_way(1, comb_piece)
    each_way(0, own_piece)
    each_way(1, own_piece)
    send_x(0)
    pass_on(0, 0)
    pass_on(1, 3)
    build_near(0, 0, 1)
    send_x(1)
    pass_on(0, 1)
    send_comb(2)
    both(3, side_copy)
    pass_on(1, 2)
    for d, i in ((0, 3), (0, 2), (1, 0), (1, 1)):
        pass_on(d, i)
    send_comb(3)
    build_near(0, 1, 3)
    finish(0)
    build_near(1, 0, 3)
    finish(1)
    send_x(2)
    build_near(3, 0, 3)
    send_x(3)
    finish(2)
    for g in range(2):
        for i in range(RING):
            arrival(part_of(g, i, 2), pass2_s.at[g, i], pass2_r.at[g, i])
    build_far(0, RING)
    forward(0)
    for dx in (0, 1, 3):
        build(mod(x + dx) * RING + mod(y + 2))
    forward(1)
    finish(3)
    gathered(0, 0)
    forward(2)
    across_copy(SLICES - 1).start()
    gathered(0, 1)
    gathered(0, 2)
    last_forward(0)
    last_forward(1)
    gathered(1, 0)
    forward(3)
    finish_out(0)
    last_forward(2)
    gathered(1, 1)
    last_forward(3)
    gathered(1, 2)
    finish_out(1)
    for t in range(GROUPS):
        receive(t)
    for i in range(A_HALF):
        value = final[pl.ds(i, NB, stride=B_STRIDE), :]
        turned = value.T.astype(BF16)
        out[:, i * NB : (i + 1) * NB] = turned[:pairs_dev]
        out[:, (i + A_HALF) * NB : (i + A_HALF + 1) * NB] = turned[pairs_dev:]

    for i in range(RING):
        swap_a(i).wait_send()
    for i in range(3):
        swap_b(i).wait_send()
    for g in range(2):
        for d in (0, 1):
            ring1(g, d).wait_send()
            half1(g, d).wait_send()
            for i in range(RING):
                ring2(g, d, i).wait_send()
        for i in range(RING):
            pass2(g, i).wait_send()
    for s in range(SLICES):
        for i in range(X_PARTS):
            x_copy(s, i).wait_send()
        for d in (0, 1):
            far_copy(s, d).wait_send()
            side_copy(s, d).wait_send()
            comb_copy(s, d).wait_send()
            ag_copy(s, d).wait_send()
            if s < SLICES - 1:
                fw_copy(s, d).wait_send()
            elif d == 0:
                across_copy(s).wait_send()
        for i in range(5):
            cx_copy(s, i).wait_send()

    for t in range(GROUPS):
        for i in FARTHEST_FIRST[0] + FARTHEST_FIRST[1]:
            out_copy(t, i).wait_send()


def on_device(tiles, owner, sub_block, fit_ac, fit_bd):
    rows_dev = tiles.shape[0]
    depth = fit_ac.shape[2]
    owner = owner.reshape(rows_dev // 128, 128)
    sub_block = sub_block.reshape(rows_dev // 128, 128)
    fit_a = fit_ac.reshape(NC * NA, depth)
    fit_b = jnp.swapaxes(fit_bd, 1, 2)
    pairs = rows_dev // TILES_PAIR * PLANE
    dma = pltpu.SemaphoreType.DMA
    return pl.pallas_call(
        kernel,
        out_shape=pltpu.VMEM((rows_dev // TILES_PAIR, NA * NB), BF16),
        in_specs=[pl.BlockSpec(memory_space=pl.ANY)] * 5,
        out_specs=pl.BlockSpec(memory_space=pltpu.VMEM),
        scratch_shapes=[
            pltpu.VMEM((NC * NA, depth), BF16),
            pltpu.VMEM((NC * NA, depth), BF16),
            pltpu.VMEM((B_CORE, depth, ND), BF16),
            pltpu.VMEM((B_CORE, depth, ND), BF16),
            pltpu.VMEM((PLANE, rows_dev + 16, ND), BF16),
            *[pltpu.VMEM((SLICES, 2, ROWS, ND), BF16)] * 6,
            *[pltpu.VMEM((SLICES, 2, ROWS, ND), F32)] * 2,
            *[pltpu.VMEM((SLICES, ROWS, ND), BF16)] * 2,
            pltpu.VMEM((SLICES, RING, CORES, 2 * NA, K_HALF), BF16),
            pltpu.VMEM((2 * RING, pairs, K_HALF), BF16),
            pltpu.VMEM((GROUPS, pairs, STEP), F32),
            *[pltpu.VMEM((GROUPS, PLANE, OUT_ROWS, 128), BF16)] * 2,
            *[pltpu.VMEM((rows_dev // 128, 128), jnp.int32)] * 2,
            pltpu.VMEM((STEP, 128), BF16),
            pltpu.VMEM((16, 128), F32),
            pltpu.VMEM((NB * B_STRIDE, 128), F32),
            dma((5,)),
            dma((7,)), dma((7,)),
            *[dma((2, 2))] * 4,
            *[dma((2, 2, RING))] * 2,
            *[dma((2, RING))] * 2,
            *[dma((SLICES, 2))] * 6,
            *[dma((SLICES, X_PARTS))] * 2,
            *[dma((SLICES, 2))] * 4,
            *[dma((SLICES, 5))] * 2,
            *[dma((GROUPS, PLANE))] * 2,
        ],
        compiler_params=pltpu.CompilerParams(
            collective_id=0, has_side_effects=True, vmem_limit_bytes=56 * 1024 * 1024
        ),
        cost_estimate=pl.CostEstimate(flops=7 * 10**9, bytes_accessed=4 * 10**6, transcendentals=0),
        name="ladder",
    )(tiles, owner, sub_block, fit_a, fit_b)


def solution(mesh):
    placed = (
        P(("blk", "occ"), None),
        P(("blk", "occ"), None),
        P(("blk", "occ")),
        P(None, None, "occ"),
        P("blk", None, "occ"),
    )
    return jax.shard_map(
        on_device, mesh=mesh, in_specs=placed, out_specs=P(("blk", "occ"), None), check_vma=False
    )
```

```python
import jax
import jax.numpy as jnp
from jax import lax
from jax.experimental import pallas as pl
from jax.experimental.pallas import tpu as pltpu
from jax.sharding import PartitionSpec as P

MESH = pl.DeviceIdType.MESH
RING = 4
CORES = 2
SLICES = 4
GROUPS = 2
TILES_PAIR = 16
NA, NB, NC, ND = 40, 128, 32, 128
BLOCKS_OWNER = 2
PLANE = RING * RING
A_HALF = NA // 2
PART = 640
C_PART = NC // RING
ROWS = C_PART * NA
B_CORE = 8
X_PARTS = 1
X_ROWS = ROWS // X_PARTS
K_HALF = C_PART * ND // 2
OUT_ROWS = 2 * CORES * A_HALF
B_STRIDE = 24
STEP = 256
FARTHEST_FIRST = ((10, 9, 6, 11, 8, 5, 7, 4), (14, 2, 15, 13, 1, 12, 3))

F32, BF16 = jnp.float32, jnp.bfloat16


def product(left, right, right_axis):
    return lax.dot_general(left, right, (((1,), (right_axis,)), ((), ())), preferred_element_type=F32)


def kernel(
    tiles, owner, sub_block, fit_a, fit_b, out,
    a_own, a_mate, b_own, b_mate, slots, far_out, side_out, comb_out, far_in, side_in, comb_in,
    keep_comb, keep_own, x_out, x_in, ints, summed, total, parcels, got, owners, subs, row_ids, names, final,
    load_sem, mate_s, mate_r, ring1_s, ring1_r, half1_s, half1_r, ring2_s, ring2_r, pass2_s, pass2_r,
    far_s, far_r, side_s, side_r, comb_s, comb_r, x_s, x_r, ag_s, ag_r, fw_s, fw_r, cx_s, cx_r, out_s, out_r,
):
    blk, occ = lax.axis_index("blk"), lax.axis_index("occ")
    x_hi, y = lax.div(blk, RING), lax.rem(blk, RING)
    z, x_lo, k = lax.div(occ, 4), lax.rem(lax.div(occ, 2), 2), lax.rem(occ, 2)
    x = x_hi * 2 + x_lo
    rows_dev = tiles.shape[0]
    pairs_dev = rows_dev // TILES_PAIR

    def mod(value):
        return lax.rem(value, RING)

    def device(x_at, y_at, z_at, k_at):
        return (lax.div(x_at, 2) * RING + y_at, z_at * 4 + lax.rem(x_at, 2) * 2 + k_at)

    up, down, far = mod(z + 1), mod(z + 3), mod(z + 2)
    mate = device(x, y, z, 1 - k)
    partner = device(x_hi * 2 + 1 - x_lo, y, z, k)

    def along(d):
        return device(x, y, mod(z + 1 + 2 * d), k)

    me = x * RING + y
    def cross(g, u_at, v_at):
        return (u_at, v_at) if g == 0 else (v_at, u_at)

    uv = (cross(0, x, y), cross(1, x, y))

    sizes = (PART, rows_dev + 16 - PART)

    def part_of(g, back_u, back_v, start=0, size=None):
        x_at, y_at = cross(g, mod(uv[g][0] + back_u), mod(uv[g][1] + back_v))
        return slots.at[x_at * RING + y_at, pl.ds(g * PART + start, sizes[g] if size is None else size)]

    def plane_device(g, ahead_u, ahead_v):
        return device(*cross(g, mod(uv[g][0] + ahead_u), mod(uv[g][1] + ahead_v)), z, k)

    def remote(src, dst, send, recv, to):
        return pltpu.make_async_remote_copy(
            src_ref=src, dst_ref=dst, send_sem=send, recv_sem=recv, device_id=to, device_id_type=MESH
        )

    def arrival(dst, send, recv):
        remote(dst, dst, send, recv, mate).wait_recv()

    load_a = pltpu.make_async_copy(fit_a, a_own, load_sem.at[0])
    load_b = pltpu.make_async_copy(fit_b.at[pl.ds(k * B_CORE, B_CORE)], b_own, load_sem.at[1])
    load_t = pltpu.make_async_copy(tiles, slots.at[me, pl.ds(0, rows_dev)], load_sem.at[2])
    load_o = pltpu.make_async_copy(owner, owners, load_sem.at[3])
    load_u = pltpu.make_async_copy(sub_block, subs, load_sem.at[4])
    for load in (load_o, load_u, load_t, load_a, load_b):
        load.start()

    barrier = pltpu.get_barrier_semaphore()

    across = device(x, y, far, k)
    for to in (mate, along(0), along(1), across):
        pl.semaphore_signal(barrier, inc=1, device_id=to, device_id_type=MESH)
    for i in range(1, PLANE):
        to = device(mod(x + i // RING), mod(y + i % RING), z, k)
        pl.semaphore_signal(barrier, inc=1, device_id=to, device_id_type=MESH)
    load_o.wait()
    load_u.wait()
    spot = (owners[...] * BLOCKS_OWNER + subs[...]) * 8 + lax.div(
        lax.broadcasted_iota(jnp.int32, owners.shape, 1), TILES_PAIR
    )
    slots[me, rows_dev : rows_dev + 16, :] = jnp.concatenate([spot, spot], axis=0).astype(F32).astype(BF16)
    row_ids[...] = lax.broadcasted_iota(jnp.int32, row_ids.shape, 0).astype(F32).astype(BF16)

    pl.semaphore_wait(barrier, PLANE + 3)

    def swap_a(i):
        rows = pl.ds(pl.multiple_of(mod(z + (2, 1, 3, 0)[i]) * ROWS, ROWS), ROWS)
        return remote(fit_a.at[rows], a_mate.at[rows], mate_s.at[i], mate_r.at[i], mate)

    def swap_b(i):
        first, count = ((0, 2), (2, 2), (4, 4))[i]
        here, there = pl.ds((1 - k) * B_CORE + first, count), pl.ds(first, count)
        return remote(fit_b.at[here], b_mate.at[there], mate_s.at[4 + i], mate_r.at[4 + i], mate)

    for swap in (swap_a(0), swap_b(0), swap_b(1), swap_a(1), swap_a(2), swap_b(2), swap_a(3)):
        swap.start()

    def ring1(g, d):
        ref = part_of(g, 0, 0)
        return remote(ref, ref, ring1_s.at[g, d], ring1_r.at[g, d], plane_device(g, 1 + 2 * d, 0))

    def half_ref(g, d, back):
        first = sizes[g] // 32 * 16
        return part_of(g, back, 0, d * first, sizes[g] - first if d else first)

    def half1(g, d):
        ref = half_ref(g, d, 3 - 2 * d)
        return remote(ref, ref, half1_s.at[g, d], half1_r.at[g, d], plane_device(g, 1 + 2 * d, 0))

    def ring2(g, d, i):
        ref = part_of(g, i, 0)
        return remote(ref, ref, ring2_s.at[g, d, i], ring2_r.at[g, d, i], plane_device(g, 0, 1 + 2 * d))

    def pass2(g, i):
        d = i // 2
        ref = part_of(g, i, 3 - 2 * d)
        return remote(ref, ref, pass2_s.at[g, i], pass2_r.at[g, i], plane_device(g, 0, 1 + 2 * d))

    def both_ways(i):
        for g in range(2):
            for d in (0, 1):
                ring2(g, d, i).start()

    def pass_on(d, i):
        for g in range(2):
            arrival(part_of(g, i, 3 - 2 * d), ring2_s.at[g, d, i], ring2_r.at[g, d, i])
            if i // 2 == d:
                pass2(g, i).start()

    load_t.wait()
    for g in range(2):
        for d in (0, 1):
            ring1(g, d).start()
    both_ways(0)
    load_a.wait()
    load_b.wait()

    def partial(part, h, t):
        rows = pl.ds(pl.multiple_of(part * ROWS, ROWS), ROWS)
        b = t * 4 + h * 2
        own = product(a_own[rows, :], jnp.concatenate([b_own[b], b_own[b + 1]], axis=1), 0)
        return own + product(a_mate[rows, :], jnp.concatenate([b_mate[b], b_mate[b + 1]], axis=1), 0)

    def far_copy(s, d):
        return remote(far_out.at[s, d], far_in.at[s, d], far_s.at[s, d], far_r.at[s, d], along(d))

    def side_copy(s, d):
        return remote(side_out.at[s, d], side_in.at[s, d], side_s.at[s, d], side_r.at[s, d], along(d))

    def comb_copy(s, d):
        return remote(comb_out.at[s, d], comb_in.at[s, d], comb_s.at[s, d], comb_r.at[s, d], along(d))

    def x_copy(s, i):
        rows = pl.ds(i * X_ROWS, X_ROWS)
        return remote(x_out.at[s, rows], x_in.at[s, rows], x_s.at[s, i], x_r.at[s, i], partner)

    def keep(ref, t, d, value):
        ref[2 * t, d] = value[:, :ND].astype(ref.dtype)
        ref[2 * t + 1, d] = value[:, ND:].astype(ref.dtype)

    def far_piece(t, d):
        keep(far_out, t, d, partial(far, d, t))

    def side_piece(t, d):
        keep(side_out, t, d, partial(mod(z + 1 + 2 * d), 1 - d, t))

    def comb_piece(t, d):
        keep(keep_comb, t, d, partial(mod(z + 1 + 2 * d), d, t))

    def own_piece(t, d):
        keep(keep_own, t, d, partial(z, d, t))

    def each_way(t, piece):
        def one(d, carry):
            piece(t, d)
            return carry

        lax.fori_loop(0, 2, one, 0)

    def both(s, copy):
        copy(s, 0).start()
        copy(s, 1).start()

    def send_comb(s):
        for d in (0, 1):
            far_copy(s, d).wait_recv()
            comb_out[s, d] = (keep_comb[s, d] + far_in[s, d].astype(F32)).astype(BF16)
            comb_copy(s, d).start()

    def build(slot):
        names[...] = slots[slot, pl.ds(rows_dev, 16), :].astype(F32)
        none = jnp.zeros((128, ND), BF16)

        def chosen(row):
            line = jnp.broadcast_to(names[row : row + 1, :], (16, 128)).astype(BF16)
            return jnp.where(row_ids[...] == jnp.concatenate([line] * 16, axis=0), 1.0, 0.0).astype(BF16)

        for j in range(rows_dev // STEP):
            choice = jnp.concatenate([chosen(2 * j), chosen(2 * j + 1)], axis=1)
            first = slots[slot, j * STEP : j * STEP + 128, :]
            second = slots[slot, j * STEP + 128 : (j + 1) * STEP, :]
            values = jnp.concatenate(
                [jnp.concatenate([first, none], axis=1), jnp.concatenate([none, second], axis=1)], axis=0
            )
            sums = product(choice, values, 0)
            rows = pl.ds(pl.multiple_of(slot * pairs_dev + j * 16, 16), 16)
            for c in range(NC):
                part = sums[c * 8 : (c + 1) * 8]
                part = jnp.concatenate([part[:, :ND], part[:, ND:]], axis=0)
                summed[c // 4, rows, (c % 4) * ND : (c % 4 + 1) * ND] = part.astype(BF16)

    def build_near(dx, first, last):
        def one(i, carry):
            build(mod(x + dx) * RING + mod(y + i + i // 2))
            return carry

        lax.fori_loop(first, last, one, 0)

    def build_far(first, last):
        def one(i, carry):
            build(mod(x + 2) * RING + mod(y + i))
            return carry

        lax.fori_loop(first, last, one, 0)

    def send_x(s):
        comb_copy(s, 0).wait_recv()
        comb_copy(s, 1).wait_recv()
        side_copy(s, 0).wait_recv()
        side_copy(s, 1).wait_recv()
        h = 1 - x_lo
        x_out[s] = (keep_own[s, h] + comb_in[s, h].astype(F32) + side_in[s, 1 - h].astype(F32)).astype(BF16)
        for i in range(X_PARTS):
            x_copy(s, i).start()

    def ag_copy(s, d):
        ref = ints.at[s, z, k]
        return remote(ref, ref, ag_s.at[s, d], ag_r.at[s, d], along(d))

    def fw_ref(s, part, core, d):
        return ints.at[s, part, core, :, pl.ds(d * STEP, STEP)]

    def fw_copy(s, d):
        ref = fw_ref(s, mod(z + 3 - 2 * d), k, d)
        return remote(ref, ref, fw_s.at[s, d], fw_r.at[s, d], along(d))

    def across_copy(s):
        ref = ints.at[s, z, k]
        return remote(ref, ref, fw_s.at[s, 0], fw_r.at[s, 0], across)

    def cx_ref(s, i, core):
        if i < 3:
            return ints.at[s, (z, down, up)[i], core]
        return fw_ref(s, far, core, i - 3)

    def cx_copy(s, i):
        ref = cx_ref(s, i, k)
        return remote(ref, ref, cx_s.at[s, i], cx_r.at[s, i], mate)

    def finish(s):
        for i in range(X_PARTS):
            x_copy(s, i).wait_recv()
        h = x_lo
        blocks = []
        for two in range(C_PART // 2):
            rows = pl.ds(two * 2 * NA, 2 * NA)
            value = (
                keep_own[s, h, rows, :]
                + comb_in[s, h, rows, :].astype(F32)
                + side_in[s, 1 - h, rows, :].astype(F32)
                + x_in[s, rows, :].astype(F32)
            )
            blocks += [value[:NA], value[NA:]]
        lines = [jnp.concatenate(blocks[i * 4 : i * 4 + 4], axis=1) for i in range(2)]
        ints[s, z, k] = jnp.concatenate(lines, axis=0).astype(BF16)
        ag_copy(s, 0).start()
        ag_copy(s, 1).start()
        cx_copy(s, 0).start()

    def forward(s):
        for d in (0, 1):
            from_z = mod(z + 3 - 2 * d)
            arrival(ints.at[s, from_z, k], ag_s.at[s, d], ag_r.at[s, d])
            if s < SLICES - 1:
                fw_copy(s, d).start()
            cx_copy(s, 1 + d).start()

    def last_forward(s):
        for d in (0, 1):
            if s < SLICES - 1:
                arrival(fw_ref(s, far, k, d), fw_s.at[s, d], fw_r.at[s, d])
            elif d == 0:
                arrival(ints.at[s, far, k], fw_s.at[s, 0], fw_r.at[s, 0])
            cx_copy(s, 3 + d).start()

    def multiply(t, part, first):
        left = [[], []]
        for s in (2 * t, 2 * t + 1):
            for core in range(CORES):
                value = ints[s, part, core].astype(F32)
                left[0].append(value[:NA])
                left[1].append(value[NA:])
        left = [jnp.concatenate(value, axis=0).astype(BF16) for value in left]

        def one(n, carry):
            rows = pl.ds(pl.multiple_of(n * 512, 512), 512)
            value = product(summed[part * 2, rows, :], left[0], 1) + product(summed[part * 2 + 1, rows, :], left[1], 1)
            total[t, rows, : 4 * NA] = value if first else total[t, rows, : 4 * NA] + value
            return carry

        lax.fori_loop(0, total.shape[1] // 512, one, 0)

    def await_gathered(t, i):
        for s in (2 * t, 2 * t + 1):
            arrival(cx_ref(s, i, 1 - k), cx_s.at[s, i], cx_r.at[s, i])
            if i == 3:
                arrival(cx_ref(s, 4, 1 - k), cx_s.at[s, 4], cx_r.at[s, 4])

    def gathered(t, i):
        await_gathered(t, i)
        multiply(t, (z, down, up, far)[i], i == 0)

    def finish_out(t):
        gathered(t, 3)
        send_out(t)

    def out_copy(t, i):
        x_at, y_at = mod(x + i // RING), mod(y + i % RING)
        return remote(
            parcels.at[t, x_at * RING + y_at], got.at[t, me], out_s.at[t, i], out_r.at[t, i], device(x_at, y_at, z, k)
        )

    def send_out(t):
        low = lax.broadcasted_iota(jnp.int32, (OUT_ROWS, 128), 1) < 64
        for n in range(PLANE // 2):
            rows = slice(n * 128, (n + 1) * 128)
            value = jnp.concatenate([total[t, rows, :128].T, total[t, rows, 128:].T[: 4 * NA - 128]], axis=0)
            top = jnp.concatenate([value[i * NA : i * NA + A_HALF] for i in range(4)], axis=0)
            bottom = jnp.concatenate([value[i * NA + A_HALF : (i + 1) * NA] for i in range(4)], axis=0)
            parcels[t, 2 * n] = jnp.where(low, top, pltpu.roll(bottom, 64, 1)).astype(BF16)
            parcels[t, 2 * n + 1] = jnp.where(low, pltpu.roll(top, 64, 1), bottom).astype(BF16)
        for i in FARTHEST_FIRST[0] + FARTHEST_FIRST[1]:
            out_copy(t, i).start()

    def unpack(t, x_at, y_at, value):
        base = (lax.div(x_at, 2) * RING + y_at) * 16 + t * 4 + lax.rem(x_at, 2) * 2
        for at in range(4):
            rows = pl.ds(pl.multiple_of((base + at % 2 * 8 + at // 2) * B_STRIDE, 8), A_HALF)
            final[rows, :] = value[at * A_HALF : (at + 1) * A_HALF]

    def receive(t):
        unpack(t, x, y, parcels[t, me].astype(F32))

        for i in FARTHEST_FIRST[0] + FARTHEST_FIRST[1]:
            x_at, y_at = mod(x + RING - i // RING), mod(y + RING - i % RING)
            slot = x_at * RING + y_at
            arrival(got.at[t, slot], out_s.at[t, i], out_r.at[t, i])
            unpack(t, x_at, y_at, got[t, slot].astype(F32))

    swap_a(0).wait_recv()
    for d in (0, 1):
        swap_b(d).wait_recv()
        far_piece(0, d)
        far_copy(0, d).start()
        far_copy(1, d).start()
    swap_a(1).wait_recv()
    swap_a(2).wait_recv()
    each_way(0, side_piece)
    both(0, side_copy)
    each_way(0, comb_piece)
    for g in range(2):
        for d in (0, 1):
            arrival(part_of(g, 3 - 2 * d, 0), ring1_s.at[g, d], ring1_r.at[g, d])
            half1(g, d).start()
    both_ways(3)
    both_ways(1)
    swap_b(2).wait_recv()
    swap_a(3).wait_recv()
    each_way(1, far_piece)
    send_comb(0)
    both(1, side_copy)
    send_comb(1)
    both(2, far_copy)
    both(3, far_copy)
    for g in range(2):
        for d in (0, 1):
            arrival(half_ref(g, d, 2), half1_s.at[g, d], half1_r.at[g, d])
    both_ways(2)
    each_way(1, side_piece)
    both(2, side_copy)
    each_way(1, comb_piece)
    each_way(0, own_piece)
    each_way(1, own_piece)
    send_x(0)
    pass_on(0, 0)
    pass_on(1, 3)
    build_near(0, 0, 1)
    send_x(1)
    pass_on(0, 1)
    send_comb(2)
    both(3, side_copy)
    pass_on(1, 2)
    for d, i in ((0, 3), (0, 2), (1, 0), (1, 1)):
        pass_on(d, i)
    send_comb(3)
    build_near(0, 1, 3)
    finish(0)
    build_near(1, 0, 3)
    finish(1)
    send_x(2)
    build_near(3, 0, 3)
    send_x(3)
    finish(2)
    for g in range(2):
        for i in range(RING):
            arrival(part_of(g, i, 2), pass2_s.at[g, i], pass2_r.at[g, i])
    build_far(0, RING)
    forward(0)
    for dx in (0, 1, 3):
        build(mod(x + dx) * RING + mod(y + 2))
    gathered(0, 0)
    forward(1)
    finish(3)
    forward(2)
    across_copy(SLICES - 1).start()
    gathered(0, 1)
    gathered(0, 2)
    last_forward(0)
    last_forward(1)
    gathered(1, 0)
    forward(3)
    finish_out(0)
    last_forward(2)
    gathered(1, 1)
    last_forward(3)
    gathered(1, 2)
    finish_out(1)
    for t in range(GROUPS):
        receive(t)
    for i in range(A_HALF):
        value = final[pl.ds(i, NB, stride=B_STRIDE), :]
        turned = value.T.astype(BF16)
        out[:, i * NB : (i + 1) * NB] = turned[:pairs_dev]
        out[:, (i + A_HALF) * NB : (i + A_HALF + 1) * NB] = turned[pairs_dev:]

    for i in range(RING):
        swap_a(i).wait_send()
    for i in range(3):
        swap_b(i).wait_send()
    for g in range(2):
        for d in (0, 1):
            ring1(g, d).wait_send()
            half1(g, d).wait_send()
            for i in range(RING):
                ring2(g, d, i).wait_send()
        for i in range(RING):
            pass2(g, i).wait_send()
    for s in range(SLICES):
        for i in range(X_PARTS):
            x_copy(s, i).wait_send()
        for d in (0, 1):
            far_copy(s, d).wait_send()
            side_copy(s, d).wait_send()
            comb_copy(s, d).wait_send()
            ag_copy(s, d).wait_send()
            if s < SLICES - 1:
                fw_copy(s, d).wait_send()
            elif d == 0:
                across_copy(s).wait_send()
        for i in range(5):
            cx_copy(s, i).wait_send()

    for t in range(GROUPS):
        for i in FARTHEST_FIRST[0] + FARTHEST_FIRST[1]:
            out_copy(t, i).wait_send()


def on_device(tiles, owner, sub_block, fit_ac, fit_bd):
    rows_dev = tiles.shape[0]
    depth = fit_ac.shape[2]
    owner = owner.reshape(rows_dev // 128, 128)
    sub_block = sub_block.reshape(rows_dev // 128, 128)
    fit_a = fit_ac.reshape(NC * NA, depth)
    fit_b = jnp.swapaxes(fit_bd, 1, 2)
    pairs = rows_dev // TILES_PAIR * PLANE
    dma = pltpu.SemaphoreType.DMA
    return pl.pallas_call(
        kernel,
        out_shape=pltpu.VMEM((rows_dev // TILES_PAIR, NA * NB), BF16),
        in_specs=[pl.BlockSpec(memory_space=pl.ANY)] * 5,
        out_specs=pl.BlockSpec(memory_space=pltpu.VMEM),
        scratch_shapes=[
            pltpu.VMEM((NC * NA, depth), BF16),
            pltpu.VMEM((NC * NA, depth), BF16),
            pltpu.VMEM((B_CORE, depth, ND), BF16),
            pltpu.VMEM((B_CORE, depth, ND), BF16),
            pltpu.VMEM((PLANE, rows_dev + 16, ND), BF16),
            *[pltpu.VMEM((SLICES, 2, ROWS, ND), BF16)] * 6,
            *[pltpu.VMEM((SLICES, 2, ROWS, ND), F32)] * 2,
            *[pltpu.VMEM((SLICES, ROWS, ND), BF16)] * 2,
            pltpu.VMEM((SLICES, RING, CORES, 2 * NA, K_HALF), BF16),
            pltpu.VMEM((2 * RING, pairs, K_HALF), BF16),
            pltpu.VMEM((GROUPS, pairs, STEP), F32),
            *[pltpu.VMEM((GROUPS, PLANE, OUT_ROWS, 128), BF16)] * 2,
            *[pltpu.VMEM((rows_dev // 128, 128), jnp.int32)] * 2,
            pltpu.VMEM((STEP, 128), BF16),
            pltpu.VMEM((16, 128), F32),
            pltpu.VMEM(((NB + 1) * B_STRIDE, 128), F32),
            dma((5,)),
            dma((7,)), dma((7,)),
            *[dma((2, 2))] * 4,
            *[dma((2, 2, RING))] * 2,
            *[dma((2, RING))] * 2,
            *[dma((SLICES, 2))] * 6,
            *[dma((SLICES, X_PARTS))] * 2,
            *[dma((SLICES, 2))] * 4,
            *[dma((SLICES, 5))] * 2,
            *[dma((GROUPS, PLANE))] * 2,
        ],
        compiler_params=pltpu.CompilerParams(
            collective_id=0, has_side_effects=True, vmem_limit_bytes=56 * 1024 * 1024
        ),
        cost_estimate=pl.CostEstimate(flops=7 * 10**9, bytes_accessed=4 * 10**6, transcendentals=0),
        name="ladder",
    )(tiles, owner, sub_block, fit_a, fit_b)


def solution(mesh):
    placed = (
        P(("blk", "occ"), None),
        P(("blk", "occ"), None),
        P(("blk", "occ")),
        P(None, None, "occ"),
        P("blk", None, "occ"),
    )
    return jax.shard_map(
        on_device, mesh=mesh, in_specs=placed, out_specs=P(("blk", "occ"), None), check_vma=False
    )
```

```python
import jax
import jax.numpy as jnp
from jax import lax
from jax.experimental import pallas as pl
from jax.experimental.pallas import tpu as pltpu
from jax.sharding import PartitionSpec as P

MESH = pl.DeviceIdType.MESH
RING = 4
CORES = 2
SLICES = 4
GROUPS = 2
TILES_PAIR = 16
NA, NB, NC, ND = 40, 128, 32, 128
BLOCKS_OWNER = 2
PLANE = RING * RING
A_HALF = NA // 2
PART = 640
C_PART = NC // RING
ROWS = C_PART * NA
B_CORE = 8
X_PARTS = 1
X_ROWS = ROWS // X_PARTS
K_HALF = C_PART * ND // 2
OUT_ROWS = 2 * CORES * A_HALF
B_STRIDE = 24
STEP = 256
FARTHEST_FIRST = ((10, 9, 6, 11, 8, 5, 7, 4), (14, 2, 15, 13, 1, 12, 3))

F32, BF16 = jnp.float32, jnp.bfloat16


def product(left, right, right_axis):
    return lax.dot_general(left, right, (((1,), (right_axis,)), ((), ())), preferred_element_type=F32)


def kernel(
    tiles, owner, sub_block, fit_a, fit_b, out,
    a_own, a_mate, b_own, b_mate, slots, far_out, side_out, comb_out, far_in, side_in, comb_in,
    keep_comb, keep_own, x_out, x_in, ints, summed, total, parcels, got, owners, subs, row_ids, names, final,
    load_sem, mate_s, mate_r, ring1_s, ring1_r, half1_s, half1_r, ring2_s, ring2_r, pass2_s, pass2_r,
    far_s, far_r, side_s, side_r, comb_s, comb_r, x_s, x_r, ag_s, ag_r, fw_s, fw_r, cx_s, cx_r, out_s, out_r,
):
    blk, occ = lax.axis_index("blk"), lax.axis_index("occ")
    x_hi, y = lax.div(blk, RING), lax.rem(blk, RING)
    z, x_lo, k = lax.div(occ, 4), lax.rem(lax.div(occ, 2), 2), lax.rem(occ, 2)
    x = x_hi * 2 + x_lo
    rows_dev = tiles.shape[0]
    pairs_dev = rows_dev // TILES_PAIR

    def mod(value):
        return lax.rem(value, RING)

    def device(x_at, y_at, z_at, k_at):
        return (lax.div(x_at, 2) * RING + y_at, z_at * 4 + lax.rem(x_at, 2) * 2 + k_at)

    up, down, far = mod(z + 1), mod(z + 3), mod(z + 2)
    mate = device(x, y, z, 1 - k)
    partner = device(x_hi * 2 + 1 - x_lo, y, z, k)

    def along(d):
        return device(x, y, mod(z + 1 + 2 * d), k)

    me = x * RING + y
    def cross(g, u_at, v_at):
        return (u_at, v_at) if g == 0 else (v_at, u_at)

    uv = (cross(0, x, y), cross(1, x, y))

    sizes = (PART, rows_dev + 16 - PART)

    def part_of(g, back_u, back_v, start=0, size=None):
        x_at, y_at = cross(g, mod(uv[g][0] + back_u), mod(uv[g][1] + back_v))
        return slots.at[x_at * RING + y_at, pl.ds(g * PART + start, sizes[g] if size is None else size)]

    def plane_device(g, ahead_u, ahead_v):
        return device(*cross(g, mod(uv[g][0] + ahead_u), mod(uv[g][1] + ahead_v)), z, k)

    def remote(src, dst, send, recv, to):
        return pltpu.make_async_remote_copy(
            src_ref=src, dst_ref=dst, send_sem=send, recv_sem=recv, device_id=to, device_id_type=MESH
        )

    def arrival(dst, send, recv):
        remote(dst, dst, send, recv, mate).wait_recv()

    load_a = pltpu.make_async_copy(fit_a, a_own, load_sem.at[0])
    load_b = pltpu.make_async_copy(fit_b.at[pl.ds(k * B_CORE, B_CORE)], b_own, load_sem.at[1])
    load_t = pltpu.make_async_copy(tiles, slots.at[me, pl.ds(0, rows_dev)], load_sem.at[2])
    load_o = pltpu.make_async_copy(owner, owners, load_sem.at[3])
    load_u = pltpu.make_async_copy(sub_block, subs, load_sem.at[4])
    for load in (load_o, load_u, load_t, load_a, load_b):
        load.start()

    barrier = pltpu.get_barrier_semaphore()

    across = device(x, y, far, k)
    for to in (mate, along(0), along(1), across):
        pl.semaphore_signal(barrier, inc=1, device_id=to, device_id_type=MESH)
    for i in range(1, PLANE):
        to = device(mod(x + i // RING), mod(y + i % RING), z, k)
        pl.semaphore_signal(barrier, inc=1, device_id=to, device_id_type=MESH)
    load_o.wait()
    load_u.wait()
    spot = (owners[...] * BLOCKS_OWNER + subs[...]) * 8 + lax.div(
        lax.broadcasted_iota(jnp.int32, owners.shape, 1), TILES_PAIR
    )
    slots[me, rows_dev : rows_dev + 16, :] = jnp.concatenate([spot, spot], axis=0).astype(F32).astype(BF16)
    row_ids[...] = lax.broadcasted_iota(jnp.int32, row_ids.shape, 0).astype(F32).astype(BF16)

    pl.semaphore_wait(barrier, PLANE + 3)

    def swap_a(i):
        rows = pl.ds(pl.multiple_of(mod(z + (2, 1, 3, 0)[i]) * ROWS, ROWS), ROWS)
        return remote(fit_a.at[rows], a_mate.at[rows], mate_s.at[i], mate_r.at[i], mate)

    def swap_b(i):
        first, count = ((0, 2), (2, 2), (4, 4))[i]
        here, there = pl.ds((1 - k) * B_CORE + first, count), pl.ds(first, count)
        return remote(fit_b.at[here], b_mate.at[there], mate_s.at[4 + i], mate_r.at[4 + i], mate)

    for swap in (swap_a(0), swap_b(0), swap_b(1), swap_a(1), swap_a(2), swap_b(2), swap_a(3)):
        swap.start()

    def ring1(g, d):
        ref = part_of(g, 0, 0)
        return remote(ref, ref, ring1_s.at[g, d], ring1_r.at[g, d], plane_device(g, 1 + 2 * d, 0))

    def half_ref(g, d, back):
        first = sizes[g] // 32 * 16
        return part_of(g, back, 0, d * first, sizes[g] - first if d else first)

    def half1(g, d):
        ref = half_ref(g, d, 3 - 2 * d)
        return remote(ref, ref, half1_s.at[g, d], half1_r.at[g, d], plane_device(g, 1 + 2 * d, 0))

    def ring2(g, d, i):
        ref = part_of(g, i, 0)
        return remote(ref, ref, ring2_s.at[g, d, i], ring2_r.at[g, d, i], plane_device(g, 0, 1 + 2 * d))

    def pass2(g, i):
        d = i // 2
        ref = part_of(g, i, 3 - 2 * d)
        return remote(ref, ref, pass2_s.at[g, i], pass2_r.at[g, i], plane_device(g, 0, 1 + 2 * d))

    def both_ways(i):
        for g in range(2):
            for d in (0, 1):
                ring2(g, d, i).start()

    def pass_on(d, i):
        for g in range(2):
            arrival(part_of(g, i, 3 - 2 * d), ring2_s.at[g, d, i], ring2_r.at[g, d, i])
            if i // 2 == d:
                pass2(g, i).start()

    load_t.wait()
    for g in range(2):
        for d in (0, 1):
            ring1(g, d).start()
    both_ways(0)
    load_a.wait()
    load_b.wait()

    def partial(part, h, t):
        rows = pl.ds(pl.multiple_of(part * ROWS, ROWS), ROWS)
        b = t * 4 + h * 2
        own = product(a_own[rows, :], jnp.concatenate([b_own[b], b_own[b + 1]], axis=1), 0)
        return own + product(a_mate[rows, :], jnp.concatenate([b_mate[b], b_mate[b + 1]], axis=1), 0)

    def far_copy(s, d):
        return remote(far_out.at[s, d], far_in.at[s, d], far_s.at[s, d], far_r.at[s, d], along(d))

    def side_copy(s, d):
        return remote(side_out.at[s, d], side_in.at[s, d], side_s.at[s, d], side_r.at[s, d], along(d))

    def comb_copy(s, d):
        return remote(comb_out.at[s, d], comb_in.at[s, d], comb_s.at[s, d], comb_r.at[s, d], along(d))

    def x_copy(s, i):
        rows = pl.ds(i * X_ROWS, X_ROWS)
        return remote(x_out.at[s, rows], x_in.at[s, rows], x_s.at[s, i], x_r.at[s, i], partner)

    def keep(ref, t, d, value):
        ref[2 * t, d] = value[:, :ND].astype(ref.dtype)
        ref[2 * t + 1, d] = value[:, ND:].astype(ref.dtype)

    def far_piece(t, d):
        keep(far_out, t, d, partial(far, d, t))

    def side_piece(t, d):
        keep(side_out, t, d, partial(mod(z + 1 + 2 * d), 1 - d, t))

    def comb_piece(t, d):
        keep(keep_comb, t, d, partial(mod(z + 1 + 2 * d), d, t))

    def own_piece(t, d):
        keep(keep_own, t, d, partial(z, d, t))

    def each_way(t, piece):
        def one(d, carry):
            piece(t, d)
            return carry

        lax.fori_loop(0, 2, one, 0)

    def both(s, copy):
        copy(s, 0).start()
        copy(s, 1).start()

    def send_comb(s):
        for d in (0, 1):
            far_copy(s, d).wait_recv()
            comb_out[s, d] = (keep_comb[s, d] + far_in[s, d].astype(F32)).astype(BF16)
            comb_copy(s, d).start()

    def build(slot):
        names[...] = slots[slot, pl.ds(rows_dev, 16), :].astype(F32)
        none = jnp.zeros((128, ND), BF16)

        def chosen(row):
            line = jnp.broadcast_to(names[row : row + 1, :], (16, 128)).astype(BF16)
            return jnp.where(row_ids[...] == jnp.concatenate([line] * 16, axis=0), 1.0, 0.0).astype(BF16)

        for j in range(rows_dev // STEP):
            choice = jnp.concatenate([chosen(2 * j), chosen(2 * j + 1)], axis=1)
            first = slots[slot, j * STEP : j * STEP + 128, :]
            second = slots[slot, j * STEP + 128 : (j + 1) * STEP, :]
            values = jnp.concatenate(
                [jnp.concatenate([first, none], axis=1), jnp.concatenate([none, second], axis=1)], axis=0
            )
            sums = product(choice, values, 0)
            rows = pl.ds(pl.multiple_of(slot * pairs_dev + j * 16, 16), 16)
            for c in range(NC):
                part = sums[c * 8 : (c + 1) * 8]
                part = jnp.concatenate([part[:, :ND], part[:, ND:]], axis=0)
                summed[c // 4, rows, (c % 4) * ND : (c % 4 + 1) * ND] = part.astype(BF16)

    def build_near(dx, first, last):
        def one(i, carry):
            build(mod(x + dx) * RING + mod(y + i + i // 2))
            return carry

        lax.fori_loop(first, last, one, 0)

    def build_far(first, last):
        def one(i, carry):
            build(mod(x + 2) * RING + mod(y + i))
            return carry

        lax.fori_loop(first, last, one, 0)

    def send_x(s):
        comb_copy(s, 0).wait_recv()
        comb_copy(s, 1).wait_recv()
        side_copy(s, 0).wait_recv()
        side_copy(s, 1).wait_recv()
        h = 1 - x_lo
        x_out[s] = (keep_own[s, h] + comb_in[s, h].astype(F32) + side_in[s, 1 - h].astype(F32)).astype(BF16)
        for i in range(X_PARTS):
            x_copy(s, i).start()

    def ag_copy(s, d):
        ref = ints.at[s, z, k]
        return remote(ref, ref, ag_s.at[s, d], ag_r.at[s, d], along(d))

    def fw_ref(s, part, core, d):
        return ints.at[s, part, core, :, pl.ds(d * STEP, STEP)]

    def fw_copy(s, d):
        ref = fw_ref(s, mod(z + 3 - 2 * d), k, d)
        return remote(ref, ref, fw_s.at[s, d], fw_r.at[s, d], along(d))

    def across_copy(s):
        ref = ints.at[s, z, k]
        return remote(ref, ref, fw_s.at[s, 0], fw_r.at[s, 0], across)

    def cx_ref(s, i, core):
        if i < 3:
            return ints.at[s, (z, down, up)[i], core]
        return fw_ref(s, far, core, i - 3)

    def cx_copy(s, i):
        ref = cx_ref(s, i, k)
        return remote(ref, ref, cx_s.at[s, i], cx_r.at[s, i], mate)

    def finish(s):
        for i in range(X_PARTS):
            x_copy(s, i).wait_recv()
        h = x_lo
        blocks = []
        for two in range(C_PART // 2):
            rows = pl.ds(two * 2 * NA, 2 * NA)
            value = (
                keep_own[s, h, rows, :]
                + comb_in[s, h, rows, :].astype(F32)
                + side_in[s, 1 - h, rows, :].astype(F32)
                + x_in[s, rows, :].astype(F32)
            )
            blocks += [value[:NA], value[NA:]]
        lines = [jnp.concatenate(blocks[i * 4 : i * 4 + 4], axis=1) for i in range(2)]
        ints[s, z, k] = jnp.concatenate(lines, axis=0).astype(BF16)
        ag_copy(s, 0).start()
        ag_copy(s, 1).start()
        cx_copy(s, 0).start()

    def forward(s):
        for d in (0, 1):
            from_z = mod(z + 3 - 2 * d)
            arrival(ints.at[s, from_z, k], ag_s.at[s, d], ag_r.at[s, d])
            if s < SLICES - 1:
                fw_copy(s, d).start()
            cx_copy(s, 1 + d).start()

    def last_forward(s):
        for d in (0, 1):
            if s < SLICES - 1:
                arrival(fw_ref(s, far, k, d), fw_s.at[s, d], fw_r.at[s, d])
            elif d == 0:
                arrival(ints.at[s, far, k], fw_s.at[s, 0], fw_r.at[s, 0])
            cx_copy(s, 3 + d).start()

    def multiply(t, parts, first):
        left = []
        for part in parts:
            values = [ints[s, part, core].astype(F32) for s in (2 * t, 2 * t + 1) for core in range(CORES)]
            left.append(jnp.concatenate([value[:NA] for value in values], axis=0).astype(BF16))
            left.append(jnp.concatenate([value[NA:] for value in values], axis=0).astype(BF16))

        def one(n, carry):
            rows = pl.ds(pl.multiple_of(n * 512, 512), 512)
            value = 0.0
            for at, part in enumerate(parts):
                for half in range(2):
                    value = value + product(summed[part * 2 + half, rows, :], left[2 * at + half], 1)
            total[t, rows, : 4 * NA] = value if first else total[t, rows, : 4 * NA] + value
            return carry

        lax.fori_loop(0, total.shape[1] // 512, one, 0)

    def gathered(t, *which):
        for i in which:
            for s in (2 * t, 2 * t + 1):
                arrival(cx_ref(s, i, 1 - k), cx_s.at[s, i], cx_r.at[s, i])
                if i == 3:
                    arrival(cx_ref(s, 4, 1 - k), cx_s.at[s, 4], cx_r.at[s, 4])
        multiply(t, [(z, down, up, far)[i] for i in which], 0 in which)

    def finish_out(t):
        gathered(t, 3)
        send_out(t)

    def out_copy(t, i):
        x_at, y_at = mod(x + i // RING), mod(y + i % RING)
        return remote(
            parcels.at[t, x_at * RING + y_at], got.at[t, me], out_s.at[t, i], out_r.at[t, i], device(x_at, y_at, z, k)
        )

    def send_out(t):
        low = lax.broadcasted_iota(jnp.int32, (OUT_ROWS, 128), 1) < 64
        for n in range(PLANE // 2):
            rows = slice(n * 128, (n + 1) * 128)
            value = jnp.concatenate([total[t, rows, :128].T, total[t, rows, 128:].T[: 4 * NA - 128]], axis=0)
            top = jnp.concatenate([value[i * NA : i * NA + A_HALF] for i in range(4)], axis=0)
            bottom = jnp.concatenate([value[i * NA + A_HALF : (i + 1) * NA] for i in range(4)], axis=0)
            parcels[t, 2 * n] = jnp.where(low, top, pltpu.roll(bottom, 64, 1)).astype(BF16)
            parcels[t, 2 * n + 1] = jnp.where(low, pltpu.roll(top, 64, 1), bottom).astype(BF16)
        for i in FARTHEST_FIRST[0] + FARTHEST_FIRST[1]:
            out_copy(t, i).start()

    def unpack(t, x_at, y_at, value):
        base = (lax.div(x_at, 2) * RING + y_at) * 16 + t * 4 + lax.rem(x_at, 2) * 2
        for at in range(4):
            rows = pl.ds(pl.multiple_of((base + at % 2 * 8 + at // 2) * B_STRIDE, 8), A_HALF)
            final[rows, :] = value[at * A_HALF : (at + 1) * A_HALF]

    def receive(t):
        unpack(t, x, y, parcels[t, me].astype(F32))

        for i in FARTHEST_FIRST[0] + FARTHEST_FIRST[1]:
            x_at, y_at = mod(x + RING - i // RING), mod(y + RING - i % RING)
            slot = x_at * RING + y_at
            arrival(got.at[t, slot], out_s.at[t, i], out_r.at[t, i])
            unpack(t, x_at, y_at, got[t, slot].astype(F32))

    swap_a(0).wait_recv()
    for d in (0, 1):
        swap_b(d).wait_recv()
        far_piece(0, d)
        far_copy(0, d).start()
        far_copy(1, d).start()
    swap_a(1).wait_recv()
    swap_a(2).wait_recv()
    each_way(0, side_piece)
    both(0, side_copy)
    each_way(0, comb_piece)
    for g in range(2):
        for d in (0, 1):
            arrival(part_of(g, 3 - 2 * d, 0), ring1_s.at[g, d], ring1_r.at[g, d])
            half1(g, d).start()
    both_ways(3)
    both_ways(1)
    swap_b(2).wait_recv()
    swap_a(3).wait_recv()
    each_way(1, far_piece)
    send_comb(0)
    both(1, side_copy)
    send_comb(1)
    both(2, far_copy)
    both(3, far_copy)
    for g in range(2):
        for d in (0, 1):
            arrival(half_ref(g, d, 2), half1_s.at[g, d], half1_r.at[g, d])
    both_ways(2)
    each_way(1, side_piece)
    both(2, side_copy)
    each_way(1, comb_piece)
    each_way(0, own_piece)
    each_way(1, own_piece)
    send_x(0)
    pass_on(0, 0)
    pass_on(1, 3)
    build_near(0, 0, 1)
    send_x(1)
    pass_on(0, 1)
    send_comb(2)
    both(3, side_copy)
    pass_on(1, 2)
    for d, i in ((0, 3), (0, 2), (1, 0), (1, 1)):
        pass_on(d, i)
    send_comb(3)
    build_near(0, 1, 3)
    finish(0)
    build_near(1, 0, 3)
    finish(1)
    send_x(2)
    build_near(3, 0, 3)
    send_x(3)
    finish(2)
    for g in range(2):
        for i in range(RING):
            arrival(part_of(g, i, 2), pass2_s.at[g, i], pass2_r.at[g, i])
    build_far(0, RING)
    forward(0)
    for dx in (0, 1, 3):
        build(mod(x + dx) * RING + mod(y + 2))
    forward(1)
    finish(3)
    gathered(0, 0)
    forward(2)
    across_copy(SLICES - 1).start()
    gathered(0, 1, 2)
    last_forward(0)
    last_forward(1)
    gathered(1, 0)
    forward(3)
    finish_out(0)
    last_forward(2)
    last_forward(3)
    gathered(1, 1, 2)
    finish_out(1)
    for t in range(GROUPS):
        receive(t)
    for i in range(A_HALF):
        value = final[pl.ds(i, NB, stride=B_STRIDE), :]
        turned = value.T.astype(BF16)
        out[:, i * NB : (i + 1) * NB] = turned[:pairs_dev]
        out[:, (i + A_HALF) * NB : (i + A_HALF + 1) * NB] = turned[pairs_dev:]

    for i in range(RING):
        swap_a(i).wait_send()
    for i in range(3):
        swap_b(i).wait_send()
    for g in range(2):
        for d in (0, 1):
            ring1(g, d).wait_send()
            half1(g, d).wait_send()
            for i in range(RING):
                ring2(g, d, i).wait_send()
        for i in range(RING):
            pass2(g, i).wait_send()
    for s in range(SLICES):
        for i in range(X_PARTS):
            x_copy(s, i).wait_send()
        for d in (0, 1):
            far_copy(s, d).wait_send()
            side_copy(s, d).wait_send()
            comb_copy(s, d).wait_send()
            ag_copy(s, d).wait_send()
            if s < SLICES - 1:
                fw_copy(s, d).wait_send()
            elif d == 0:
                across_copy(s).wait_send()
        for i in range(5):
            cx_copy(s, i).wait_send()

    for t in range(GROUPS):
        for i in FARTHEST_FIRST[0] + FARTHEST_FIRST[1]:
            out_copy(t, i).wait_send()


def on_device(tiles, owner, sub_block, fit_ac, fit_bd):
    rows_dev = tiles.shape[0]
    depth = fit_ac.shape[2]
    owner = owner.reshape(rows_dev // 128, 128)
    sub_block = sub_block.reshape(rows_dev // 128, 128)
    fit_a = fit_ac.reshape(NC * NA, depth)
    fit_b = jnp.swapaxes(fit_bd, 1, 2)
    pairs = rows_dev // TILES_PAIR * PLANE
    dma = pltpu.SemaphoreType.DMA
    return pl.pallas_call(
        kernel,
        out_shape=pltpu.VMEM((rows_dev // TILES_PAIR, NA * NB), BF16),
        in_specs=[pl.BlockSpec(memory_space=pl.ANY)] * 5,
        out_specs=pl.BlockSpec(memory_space=pltpu.VMEM),
        scratch_shapes=[
            pltpu.VMEM((NC * NA, depth), BF16),
            pltpu.VMEM((NC * NA, depth), BF16),
            pltpu.VMEM((B_CORE, depth, ND), BF16),
            pltpu.VMEM((B_CORE, depth, ND), BF16),
            pltpu.VMEM((PLANE, rows_dev + 16, ND), BF16),
            *[pltpu.VMEM((SLICES, 2, ROWS, ND), BF16)] * 6,
            *[pltpu.VMEM((SLICES, 2, ROWS, ND), F32)] * 2,
            *[pltpu.VMEM((SLICES, ROWS, ND), BF16)] * 2,
            pltpu.VMEM((SLICES, RING, CORES, 2 * NA, K_HALF), BF16),
            pltpu.VMEM((2 * RING, pairs, K_HALF), BF16),
            pltpu.VMEM((GROUPS, pairs, STEP), F32),
            *[pltpu.VMEM((GROUPS, PLANE, OUT_ROWS, 128), BF16)] * 2,
            *[pltpu.VMEM((rows_dev // 128, 128), jnp.int32)] * 2,
            pltpu.VMEM((STEP, 128), BF16),
            pltpu.VMEM((16, 128), F32),
            pltpu.VMEM(((NB + 1) * B_STRIDE, 128), F32),
            dma((5,)),
            dma((7,)), dma((7,)),
            *[dma((2, 2))] * 4,
            *[dma((2, 2, RING))] * 2,
            *[dma((2, RING))] * 2,
            *[dma((SLICES, 2))] * 6,
            *[dma((SLICES, X_PARTS))] * 2,
            *[dma((SLICES, 2))] * 4,
            *[dma((SLICES, 5))] * 2,
            *[dma((GROUPS, PLANE))] * 2,
        ],
        compiler_params=pltpu.CompilerParams(
            collective_id=0, has_side_effects=True, vmem_limit_bytes=56 * 1024 * 1024
        ),
        cost_estimate=pl.CostEstimate(flops=7 * 10**9, bytes_accessed=4 * 10**6, transcendentals=0),
        name="ladder",
    )(tiles, owner, sub_block, fit_a, fit_b)


def solution(mesh):
    placed = (
        P(("blk", "occ"), None),
        P(("blk", "occ"), None),
        P(("blk", "occ")),
        P(None, None, "occ"),
        P("blk", None, "occ"),
    )
    return jax.shard_map(
        on_device, mesh=mesh, in_specs=placed, out_specs=P(("blk", "occ"), None), check_vma=False
    )
```

```python
import jax
import jax.numpy as jnp
from jax import lax
from jax.experimental import pallas as pl
from jax.experimental.pallas import tpu as pltpu
from jax.sharding import PartitionSpec as P

MESH = pl.DeviceIdType.MESH
RING = 4
CORES = 2
SLICES = 4
GROUPS = 2
TILES_PAIR = 16
NA, NB, NC, ND = 40, 128, 32, 128
BLOCKS_OWNER = 2
PLANE = RING * RING
A_HALF = NA // 2
PART = 640
C_PART = NC // RING
ROWS = C_PART * NA
B_CORE = 8
X_PARTS = 1
X_ROWS = ROWS // X_PARTS
K_HALF = C_PART * ND // 2
OUT_ROWS = 2 * CORES * A_HALF
B_STRIDE = 24
STEP = 256
FARTHEST_FIRST = ((10, 9, 6, 11, 8, 5, 7, 4), (14, 2, 15, 13, 1, 12, 3))

F32, BF16 = jnp.float32, jnp.bfloat16


def product(left, right, right_axis):
    return lax.dot_general(left, right, (((1,), (right_axis,)), ((), ())), preferred_element_type=F32)


def kernel(
    tiles, owner, sub_block, fit_a, fit_b, out,
    a_own, a_mate, b_own, b_mate, slots, far_out, side_out, comb_out, far_in, side_in, comb_in,
    keep_comb, keep_own, x_out, x_in, ints, summed, total, parcels, got, owners, subs, row_ids, names, final, begun,
    load_sem, mate_s, mate_r, ring1_s, ring1_r, half1_s, half1_r, ring2_s, ring2_r, pass2_s, pass2_r,
    far_s, far_r, side_s, side_r, comb_s, comb_r, x_s, x_r, ag_s, ag_r, fw_s, fw_r, cx_s, cx_r, out_s, out_r,
):
    blk, occ = lax.axis_index("blk"), lax.axis_index("occ")
    x_hi, y = lax.div(blk, RING), lax.rem(blk, RING)
    z, x_lo, k = lax.div(occ, 4), lax.rem(lax.div(occ, 2), 2), lax.rem(occ, 2)
    x = x_hi * 2 + x_lo
    rows_dev = tiles.shape[0]
    pairs_dev = rows_dev // TILES_PAIR

    def mod(value):
        return lax.rem(value, RING)

    def device(x_at, y_at, z_at, k_at):
        return (lax.div(x_at, 2) * RING + y_at, z_at * 4 + lax.rem(x_at, 2) * 2 + k_at)

    up, down, far = mod(z + 1), mod(z + 3), mod(z + 2)
    mate = device(x, y, z, 1 - k)
    partner = device(x_hi * 2 + 1 - x_lo, y, z, k)

    def along(d):
        return device(x, y, mod(z + 1 + 2 * d), k)

    me = x * RING + y
    def cross(g, u_at, v_at):
        return (u_at, v_at) if g == 0 else (v_at, u_at)

    uv = (cross(0, x, y), cross(1, x, y))

    sizes = (PART, rows_dev + 16 - PART)

    def part_of(g, back_u, back_v, start=0, size=None):
        x_at, y_at = cross(g, mod(uv[g][0] + back_u), mod(uv[g][1] + back_v))
        return slots.at[x_at * RING + y_at, pl.ds(g * PART + start, sizes[g] if size is None else size)]

    def plane_device(g, ahead_u, ahead_v):
        return device(*cross(g, mod(uv[g][0] + ahead_u), mod(uv[g][1] + ahead_v)), z, k)

    def remote(src, dst, send, recv, to):
        return pltpu.make_async_remote_copy(
            src_ref=src, dst_ref=dst, send_sem=send, recv_sem=recv, device_id=to, device_id_type=MESH
        )

    def arrival(dst, send, recv):
        remote(dst, dst, send, recv, mate).wait_recv()

    load_a = pltpu.make_async_copy(fit_a, a_own, load_sem.at[0])
    load_b = pltpu.make_async_copy(fit_b.at[pl.ds(k * B_CORE, B_CORE)], b_own, load_sem.at[1])
    load_t = pltpu.make_async_copy(tiles, slots.at[me, pl.ds(0, rows_dev)], load_sem.at[2])
    load_o = pltpu.make_async_copy(owner, owners, load_sem.at[3])
    load_u = pltpu.make_async_copy(sub_block, subs, load_sem.at[4])
    for load in (load_o, load_u, load_t, load_a, load_b):
        load.start()

    barrier = pltpu.get_barrier_semaphore()

    across = device(x, y, far, k)
    for to in (mate, along(0), along(1), across):
        pl.semaphore_signal(barrier, inc=1, device_id=to, device_id_type=MESH)
    for i in range(1, PLANE):
        to = device(mod(x + i // RING), mod(y + i % RING), z, k)
        pl.semaphore_signal(barrier, inc=1, device_id=to, device_id_type=MESH)
    load_o.wait()
    load_u.wait()
    spot = (owners[...] * BLOCKS_OWNER + subs[...]) * 8 + lax.div(
        lax.broadcasted_iota(jnp.int32, owners.shape, 1), TILES_PAIR
    )
    slots[me, rows_dev : rows_dev + 16, :] = jnp.concatenate([spot, spot], axis=0).astype(F32).astype(BF16)
    row_ids[...] = lax.broadcasted_iota(jnp.int32, row_ids.shape, 0).astype(F32).astype(BF16)

    load_a.wait()
    load_b.wait()

    def share(left, right, part, h, t):
        rows = pl.ds(pl.multiple_of(part * ROWS, ROWS), ROWS)
        b = t * 4 + h * 2
        return product(left[rows, :], jnp.concatenate([right[b], right[b + 1]], axis=1), 0)

    def partial(part, h, t):
        return share(a_own, b_own, part, h, t) + share(a_mate, b_mate, part, h, t)

    def begin(d, carry):
        begun[d] = share(a_own, b_own, far, d, 0)
        return carry

    lax.fori_loop(0, 2, begin, 0)
    pl.semaphore_wait(barrier, PLANE + 3)

    def swap_a(i):
        rows = pl.ds(pl.multiple_of(mod(z + (2, 1, 3, 0)[i]) * ROWS, ROWS), ROWS)
        return remote(fit_a.at[rows], a_mate.at[rows], mate_s.at[i], mate_r.at[i], mate)

    def swap_b(i):
        first, count = ((0, 2), (2, 2), (4, 4))[i]
        here, there = pl.ds((1 - k) * B_CORE + first, count), pl.ds(first, count)
        return remote(fit_b.at[here], b_mate.at[there], mate_s.at[4 + i], mate_r.at[4 + i], mate)

    for swap in (swap_a(0), swap_b(0), swap_b(1), swap_a(1), swap_a(2), swap_b(2), swap_a(3)):
        swap.start()

    def ring1(g, d):
        ref = part_of(g, 0, 0)
        return remote(ref, ref, ring1_s.at[g, d], ring1_r.at[g, d], plane_device(g, 1 + 2 * d, 0))

    def half_ref(g, d, back):
        first = sizes[g] // 32 * 16
        return part_of(g, back, 0, d * first, sizes[g] - first if d else first)

    def half1(g, d):
        ref = half_ref(g, d, 3 - 2 * d)
        return remote(ref, ref, half1_s.at[g, d], half1_r.at[g, d], plane_device(g, 1 + 2 * d, 0))

    def ring2(g, d, i):
        ref = part_of(g, i, 0)
        return remote(ref, ref, ring2_s.at[g, d, i], ring2_r.at[g, d, i], plane_device(g, 0, 1 + 2 * d))

    def pass2(g, i):
        d = i // 2
        ref = part_of(g, i, 3 - 2 * d)
        return remote(ref, ref, pass2_s.at[g, i], pass2_r.at[g, i], plane_device(g, 0, 1 + 2 * d))

    def both_ways(i):
        for g in range(2):
            for d in (0, 1):
                ring2(g, d, i).start()

    def pass_on(d, i):
        for g in range(2):
            arrival(part_of(g, i, 3 - 2 * d), ring2_s.at[g, d, i], ring2_r.at[g, d, i])
            if i // 2 == d:
                pass2(g, i).start()

    load_t.wait()
    for g in range(2):
        for d in (0, 1):
            ring1(g, d).start()
    both_ways(0)

    def far_copy(s, d):
        return remote(far_out.at[s, d], far_in.at[s, d], far_s.at[s, d], far_r.at[s, d], along(d))

    def side_copy(s, d):
        return remote(side_out.at[s, d], side_in.at[s, d], side_s.at[s, d], side_r.at[s, d], along(d))

    def comb_copy(s, d):
        return remote(comb_out.at[s, d], comb_in.at[s, d], comb_s.at[s, d], comb_r.at[s, d], along(d))

    def x_copy(s, i):
        rows = pl.ds(i * X_ROWS, X_ROWS)
        return remote(x_out.at[s, rows], x_in.at[s, rows], x_s.at[s, i], x_r.at[s, i], partner)

    def keep(ref, t, d, value):
        ref[2 * t, d] = value[:, :ND].astype(ref.dtype)
        ref[2 * t + 1, d] = value[:, ND:].astype(ref.dtype)

    def far_piece(t, d):
        keep(far_out, t, d, partial(far, d, t))

    def side_piece(t, d):
        keep(side_out, t, d, partial(mod(z + 1 + 2 * d), 1 - d, t))

    def comb_piece(t, d):
        keep(keep_comb, t, d, partial(mod(z + 1 + 2 * d), d, t))

    def own_piece(t, d):
        keep(keep_own, t, d, partial(z, d, t))

    def each_way(t, piece):
        def one(d, carry):
            piece(t, d)
            return carry

        lax.fori_loop(0, 2, one, 0)

    def both(s, copy):
        copy(s, 0).start()
        copy(s, 1).start()

    def send_comb(s):
        for d in (0, 1):
            far_copy(s, d).wait_recv()
            comb_out[s, d] = (keep_comb[s, d] + far_in[s, d].astype(F32)).astype(BF16)
            comb_copy(s, d).start()

    def build(slot):
        names[...] = slots[slot, pl.ds(rows_dev, 16), :].astype(F32)
        none = jnp.zeros((128, ND), BF16)

        def chosen(row):
            line = jnp.broadcast_to(names[row : row + 1, :], (16, 128)).astype(BF16)
            return jnp.where(row_ids[...] == jnp.concatenate([line] * 16, axis=0), 1.0, 0.0).astype(BF16)

        for j in range(rows_dev // STEP):
            choice = jnp.concatenate([chosen(2 * j), chosen(2 * j + 1)], axis=1)
            first = slots[slot, j * STEP : j * STEP + 128, :]
            second = slots[slot, j * STEP + 128 : (j + 1) * STEP, :]
            values = jnp.concatenate(
                [jnp.concatenate([first, none], axis=1), jnp.concatenate([none, second], axis=1)], axis=0
            )
            sums = product(choice, values, 0)
            rows = pl.ds(pl.multiple_of(slot * pairs_dev + j * 16, 16), 16)
            for c in range(NC):
                part = sums[c * 8 : (c + 1) * 8]
                part = jnp.concatenate([part[:, :ND], part[:, ND:]], axis=0)
                summed[c // 4, rows, (c % 4) * ND : (c % 4 + 1) * ND] = part.astype(BF16)

    def build_near(dx, first, last):
        def one(i, carry):
            build(mod(x + dx) * RING + mod(y + i + i // 2))
            return carry

        lax.fori_loop(first, last, one, 0)

    def build_far(first, last):
        def one(i, carry):
            build(mod(x + 2) * RING + mod(y + i))
            return carry

        lax.fori_loop(first, last, one, 0)

    def send_x(s):
        comb_copy(s, 0).wait_recv()
        comb_copy(s, 1).wait_recv()
        side_copy(s, 0).wait_recv()
        side_copy(s, 1).wait_recv()
        h = 1 - x_lo
        x_out[s] = (keep_own[s, h] + comb_in[s, h].astype(F32) + side_in[s, 1 - h].astype(F32)).astype(BF16)
        for i in range(X_PARTS):
            x_copy(s, i).start()

    def ag_copy(s, d):
        ref = ints.at[s, z, k]
        return remote(ref, ref, ag_s.at[s, d], ag_r.at[s, d], along(d))

    def fw_ref(s, part, core, d):
        return ints.at[s, part, core, :, pl.ds(d * STEP, STEP)]

    def fw_copy(s, d):
        ref = fw_ref(s, mod(z + 3 - 2 * d), k, d)
        return remote(ref, ref, fw_s.at[s, d], fw_r.at[s, d], along(d))

    def across_copy(s):
        ref = ints.at[s, z, k]
        return remote(ref, ref, fw_s.at[s, 0], fw_r.at[s, 0], across)

    def cx_ref(s, i, core):
        if i < 3:
            return ints.at[s, (z, down, up)[i], core]
        return fw_ref(s, far, core, i - 3)

    def cx_copy(s, i):
        ref = cx_ref(s, i, k)
        return remote(ref, ref, cx_s.at[s, i], cx_r.at[s, i], mate)

    def finish(s):
        for i in range(X_PARTS):
            x_copy(s, i).wait_recv()
        h = x_lo
        blocks = []
        for two in range(C_PART // 2):
            rows = pl.ds(two * 2 * NA, 2 * NA)
            value = (
                keep_own[s, h, rows, :]
                + comb_in[s, h, rows, :].astype(F32)
                + side_in[s, 1 - h, rows, :].astype(F32)
                + x_in[s, rows, :].astype(F32)
            )
            blocks += [value[:NA], value[NA:]]
        lines = [jnp.concatenate(blocks[i * 4 : i * 4 + 4], axis=1) for i in range(2)]
        ints[s, z, k] = jnp.concatenate(lines, axis=0).astype(BF16)
        ag_copy(s, 0).start()
        ag_copy(s, 1).start()
        cx_copy(s, 0).start()

    def forward(s):
        for d in (0, 1):
            from_z = mod(z + 3 - 2 * d)
            arrival(ints.at[s, from_z, k], ag_s.at[s, d], ag_r.at[s, d])
            if s < SLICES - 1:
                fw_copy(s, d).start()
            cx_copy(s, 1 + d).start()

    def last_forward(s):
        for d in (0, 1):
            if s < SLICES - 1:
                arrival(fw_ref(s, far, k, d), fw_s.at[s, d], fw_r.at[s, d])
            elif d == 0:
                arrival(ints.at[s, far, k], fw_s.at[s, 0], fw_r.at[s, 0])
            cx_copy(s, 3 + d).start()

    def multiply(t, parts, first):
        left = []
        for part in parts:
            values = [ints[s, part, core].astype(F32) for s in (2 * t, 2 * t + 1) for core in range(CORES)]
            left.append(jnp.concatenate([value[:NA] for value in values], axis=0).astype(BF16))
            left.append(jnp.concatenate([value[NA:] for value in values], axis=0).astype(BF16))

        def one(n, carry):
            rows = pl.ds(pl.multiple_of(n * 512, 512), 512)
            value = 0.0
            for at, part in enumerate(parts):
                for half in range(2):
                    value = value + product(summed[part * 2 + half, rows, :], left[2 * at + half], 1)
            total[t, rows, : 4 * NA] = value if first else total[t, rows, : 4 * NA] + value
            return carry

        lax.fori_loop(0, total.shape[1] // 512, one, 0)

    def gathered(t, *which):
        for i in which:
            for s in (2 * t, 2 * t + 1):
                arrival(cx_ref(s, i, 1 - k), cx_s.at[s, i], cx_r.at[s, i])
                if i == 3:
                    arrival(cx_ref(s, 4, 1 - k), cx_s.at[s, 4], cx_r.at[s, 4])
        multiply(t, [(z, down, up, far)[i] for i in which], 0 in which)

    def finish_out(t):
        gathered(t, 3)
        send_out(t)

    def out_copy(t, i):
        x_at, y_at = mod(x + i // RING), mod(y + i % RING)
        return remote(
            parcels.at[t, x_at * RING + y_at], got.at[t, me], out_s.at[t, i], out_r.at[t, i], device(x_at, y_at, z, k)
        )

    def send_out(t):
        low = lax.broadcasted_iota(jnp.int32, (OUT_ROWS, 128), 1) < 64
        for n in range(PLANE // 2):
            rows = slice(n * 128, (n + 1) * 128)
            value = jnp.concatenate([total[t, rows, :128].T, total[t, rows, 128:].T[: 4 * NA - 128]], axis=0)
            top = jnp.concatenate([value[i * NA : i * NA + A_HALF] for i in range(4)], axis=0)
            bottom = jnp.concatenate([value[i * NA + A_HALF : (i + 1) * NA] for i in range(4)], axis=0)
            parcels[t, 2 * n] = jnp.where(low, top, pltpu.roll(bottom, 64, 1)).astype(BF16)
            parcels[t, 2 * n + 1] = jnp.where(low, pltpu.roll(top, 64, 1), bottom).astype(BF16)
        for i in FARTHEST_FIRST[0] + FARTHEST_FIRST[1]:
            out_copy(t, i).start()

    def unpack(t, x_at, y_at, value):
        base = (lax.div(x_at, 2) * RING + y_at) * 16 + t * 4 + lax.rem(x_at, 2) * 2
        for at in range(4):
            rows = pl.ds(pl.multiple_of((base + at % 2 * 8 + at // 2) * B_STRIDE, 8), A_HALF)
            final[rows, :] = value[at * A_HALF : (at + 1) * A_HALF]

    def receive(t):
        unpack(t, x, y, parcels[t, me].astype(F32))

        for i in FARTHEST_FIRST[0] + FARTHEST_FIRST[1]:
            x_at, y_at = mod(x + RING - i // RING), mod(y + RING - i % RING)
            slot = x_at * RING + y_at
            arrival(got.at[t, slot], out_s.at[t, i], out_r.at[t, i])
            unpack(t, x_at, y_at, got[t, slot].astype(F32))

    swap_a(0).wait_recv()
    for d in (0, 1):
        swap_b(d).wait_recv()
        keep(far_out, 0, d, begun[d] + share(a_mate, b_mate, far, d, 0))
        far_copy(0, d).start()
        far_copy(1, d).start()
    swap_a(1).wait_recv()
    swap_a(2).wait_recv()
    each_way(0, side_piece)
    both(0, side_copy)
    each_way(0, comb_piece)
    for g in range(2):
        for d in (0, 1):
            arrival(part_of(g, 3 - 2 * d, 0), ring1_s.at[g, d], ring1_r.at[g, d])
            half1(g, d).start()
    both_ways(3)
    both_ways(1)
    swap_b(2).wait_recv()
    swap_a(3).wait_recv()
    each_way(1, far_piece)
    send_comb(0)
    both(1, side_copy)
    send_comb(1)
    both(2, far_copy)
    both(3, far_copy)
    for g in range(2):
        for d in (0, 1):
            arrival(half_ref(g, d, 2), half1_s.at[g, d], half1_r.at[g, d])
    both_ways(2)
    each_way(1, side_piece)
    both(2, side_copy)
    each_way(1, comb_piece)
    each_way(0, own_piece)
    each_way(1, own_piece)
    send_x(0)
    pass_on(0, 0)
    pass_on(1, 3)
    build_near(0, 0, 1)
    send_x(1)
    pass_on(0, 1)
    send_comb(2)
    both(3, side_copy)
    pass_on(1, 2)
    for d, i in ((0, 3), (0, 2), (1, 0), (1, 1)):
        pass_on(d, i)
    send_comb(3)
    build_near(0, 1, 3)
    finish(0)
    build_near(1, 0, 3)
    finish(1)
    send_x(2)
    build_near(3, 0, 3)
    send_x(3)
    finish(2)
    for g in range(2):
        for i in range(RING):
            arrival(part_of(g, i, 2), pass2_s.at[g, i], pass2_r.at[g, i])
    build_far(0, RING)
    forward(0)
    for dx in (0, 1, 3):
        build(mod(x + dx) * RING + mod(y + 2))
    forward(1)
    finish(3)
    gathered(0, 0)
    forward(2)
    across_copy(SLICES - 1).start()
    gathered(0, 1, 2)
    last_forward(0)
    last_forward(1)
    gathered(1, 0)
    forward(3)
    finish_out(0)
    last_forward(2)
    last_forward(3)
    gathered(1, 1, 2)
    finish_out(1)
    for t in range(GROUPS):
        receive(t)
    for i in range(A_HALF):
        value = final[pl.ds(i, NB, stride=B_STRIDE), :]
        turned = value.T.astype(BF16)
        out[:, i * NB : (i + 1) * NB] = turned[:pairs_dev]
        out[:, (i + A_HALF) * NB : (i + A_HALF + 1) * NB] = turned[pairs_dev:]

    for i in range(RING):
        swap_a(i).wait_send()
    for i in range(3):
        swap_b(i).wait_send()
    for g in range(2):
        for d in (0, 1):
            ring1(g, d).wait_send()
            half1(g, d).wait_send()
            for i in range(RING):
                ring2(g, d, i).wait_send()
        for i in range(RING):
            pass2(g, i).wait_send()
    for s in range(SLICES):
        for i in range(X_PARTS):
            x_copy(s, i).wait_send()
        for d in (0, 1):
            far_copy(s, d).wait_send()
            side_copy(s, d).wait_send()
            comb_copy(s, d).wait_send()
            ag_copy(s, d).wait_send()
            if s < SLICES - 1:
                fw_copy(s, d).wait_send()
            elif d == 0:
                across_copy(s).wait_send()
        for i in range(5):
            cx_copy(s, i).wait_send()

    for t in range(GROUPS):
        for i in FARTHEST_FIRST[0] + FARTHEST_FIRST[1]:
            out_copy(t, i).wait_send()


def on_device(tiles, owner, sub_block, fit_ac, fit_bd):
    rows_dev = tiles.shape[0]
    depth = fit_ac.shape[2]
    owner = owner.reshape(rows_dev // 128, 128)
    sub_block = sub_block.reshape(rows_dev // 128, 128)
    fit_a = fit_ac.reshape(NC * NA, depth)
    fit_b = jnp.swapaxes(fit_bd, 1, 2)
    pairs = rows_dev // TILES_PAIR * PLANE
    dma = pltpu.SemaphoreType.DMA
    return pl.pallas_call(
        kernel,
        out_shape=pltpu.VMEM((rows_dev // TILES_PAIR, NA * NB), BF16),
        in_specs=[pl.BlockSpec(memory_space=pl.ANY)] * 5,
        out_specs=pl.BlockSpec(memory_space=pltpu.VMEM),
        scratch_shapes=[
            pltpu.VMEM((NC * NA, depth), BF16),
            pltpu.VMEM((NC * NA, depth), BF16),
            pltpu.VMEM((B_CORE, depth, ND), BF16),
            pltpu.VMEM((B_CORE, depth, ND), BF16),
            pltpu.VMEM((PLANE, rows_dev + 16, ND), BF16),
            *[pltpu.VMEM((SLICES, 2, ROWS, ND), BF16)] * 6,
            *[pltpu.VMEM((SLICES, 2, ROWS, ND), F32)] * 2,
            *[pltpu.VMEM((SLICES, ROWS, ND), BF16)] * 2,
            pltpu.VMEM((SLICES, RING, CORES, 2 * NA, K_HALF), BF16),
            pltpu.VMEM((2 * RING, pairs, K_HALF), BF16),
            pltpu.VMEM((GROUPS, pairs, STEP), F32),
            *[pltpu.VMEM((GROUPS, PLANE, OUT_ROWS, 128), BF16)] * 2,
            *[pltpu.VMEM((rows_dev // 128, 128), jnp.int32)] * 2,
            pltpu.VMEM((STEP, 128), BF16),
            pltpu.VMEM((16, 128), F32),
            pltpu.VMEM(((NB + 1) * B_STRIDE, 128), F32),
            pltpu.VMEM((2, ROWS, 2 * ND), F32),
            dma((5,)),
            dma((7,)), dma((7,)),
            *[dma((2, 2))] * 4,
            *[dma((2, 2, RING))] * 2,
            *[dma((2, RING))] * 2,
            *[dma((SLICES, 2))] * 6,
            *[dma((SLICES, X_PARTS))] * 2,
            *[dma((SLICES, 2))] * 4,
            *[dma((SLICES, 5))] * 2,
            *[dma((GROUPS, PLANE))] * 2,
        ],
        compiler_params=pltpu.CompilerParams(
            collective_id=0, has_side_effects=True, vmem_limit_bytes=56 * 1024 * 1024
        ),
        cost_estimate=pl.CostEstimate(flops=7 * 10**9, bytes_accessed=4 * 10**6, transcendentals=0),
        name="ladder",
    )(tiles, owner, sub_block, fit_a, fit_b)


def solution(mesh):
    placed = (
        P(("blk", "occ"), None),
        P(("blk", "occ"), None),
        P(("blk", "occ")),
        P(None, None, "occ"),
        P("blk", None, "occ"),
    )
    return jax.shard_map(
        on_device, mesh=mesh, in_specs=placed, out_specs=P(("blk", "occ"), None), check_vma=False
    )
```
